128 devices in a mesh: group: 4 (over y_lo, core), fsdp: 32 (over y_hi, x, z).
Axes of the slice: x: 4, y: 4 (y_hi: 2, y_lo: 2; y = y_hi * 2 + y_lo), z: 4, core: 2. Of those that a mesh axis runs over, the one named last changes fastest.
Arguments:
- grads: float32 [128, 4, 1048576], P(('group', 'fsdp')), may hold values from -24 to 24
- params: float32 [4, 1048576], P('group', 'fsdp'), may hold values from -6 to 6
- moment_one: float32 [4, 1048576], P('group', 'fsdp'), may hold values from -18 to 18
- moment_two: float32 [4, 1048576], P('group', 'fsdp'), may hold values from 1 to 100
- coding: float32 [4, 2], replicated, as said below
- holders: int32 [32, 2], P('fsdp'), may hold values from 0 to 3, as said below
Outputs:
- new_params: float32 [4, 1048576], P('group', 'fsdp')
- new_moment_one: float32 [4, 1048576], P('group', 'fsdp')
- new_moment_two: float32 [4, 1048576], P('group', 'fsdp')
- parity_held: float32 [4, 1048576], P('group', 'fsdp')
The draws below stay inside these ranges and needn't reach their ends.
Inputs may be any that keep to these rules, and one draw needn't show every extreme that they name: `holders`: the two groups of a slot differ. coding[g, k] = 1 / (x_g + y_k) with distinct positive x_g and y_k.
All inputs are finite; a program needn't handle non-finite values.
Results may differ from the reference program's by a relative error of at most 0.000071.
Values sent between devices are 32-bit elements; how exact they have to be, the bound alone decides.
A program may use at most 128 MiB of HBM per device.

```python
import math
import jax
import jax.numpy as jnp
from jax import lax

SHARD = 32768
GROUPS = 4
SLOTS = 32
CONTRIB = 128


def draw_coding(key, part):
    key = jax.random.fold_in(key, 11)
    first_key, second_key = jax.random.split(key)
    group_points = jnp.arange(GROUPS, dtype=jnp.float32) + jax.random.uniform(first_key, (GROUPS,), jnp.float32, 0.2, 0.8)
    parity_points = 0.5 * jnp.arange(2, dtype=jnp.float32) + jax.random.uniform(second_key, (2,), jnp.float32, 0.1, 0.4)
    return 1.0 / (group_points[:, None] + parity_points[None, :] + 0.5)


def draw_holders(key, part):
    key = jax.random.fold_in(key, 23)
    first_key, second_key = jax.random.split(key)
    leading = jax.random.randint(first_key, (SLOTS,), 0, GROUPS)
    distance = jax.random.randint(second_key, (SLOTS,), 1, GROUPS)
    partner = (leading + distance) % GROUPS
    return jnp.stack([leading, partner], axis=1).astype(jnp.int32)


def raised(drawn, rng, source, target, blocks, factor):
    owner, partner = [(jnp.arange(drawn.shape[position]) // (drawn.shape[position] // blocks)).reshape([-1 if axis == position else 1 for axis in range(drawn.ndim)]) for position in (source, target)]
    chosen = jax.random.permutation(rng, blocks)[partner]
    strong = (owner == chosen) | (owner == (partner + blocks // 2) % blocks)
    return jnp.where(strong, factor * drawn, drawn)


def shard_levels(key, dims, pieces, smallest, top_value):
    loudness = 1.0
    for dim, parts in pieces:
        heights = jax.random.uniform(jax.random.fold_in(jax.random.fold_in(key, 6), dim), (parts,), jnp.float32, smallest / len(pieces), top_value / len(pieces))
        loudness = loudness * jnp.repeat(jnp.exp(heights), dims[dim] // parts).reshape((-1,) + (1,) * (len(dims) - 1 - dim))
    return loudness


def normal_values(key, dims, width, bound, pieces=(), held_as=jnp.bfloat16):
    values = jax.random.normal(key, dims, jnp.float32) * width
    if len(pieces) > 0:
        values = shard_levels(key, dims, pieces, -0.22, 0.18) * values
    return jnp.clip(values, min=-bound, max=bound).astype(held_as)


def noise_with(stream_key, dims, spread, most, cuts, heavy, kind=jnp.bfloat16):
    entries = spread * jax.random.normal(stream_key, dims, jnp.float32)
    if cuts:
        entries = entries * shard_levels(stream_key, dims, cuts, -0.22, 0.18)
    return jnp.clip(raised(entries, jax.random.fold_in(stream_key, 3), *heavy), -most, most).astype(kind)


def setup_inputs(seed: int = 0) -> dict:
    key_of = jax.random.split(jax.random.key(seed), 7)
    grads = noise_with(key_of[0], (CONTRIB, GROUPS, SLOTS * SHARD), 1.0, 24.0, ((0, 128),), (0, 2, 128, 5.5), jnp.float32)
    params = normal_values(key_of[1], (GROUPS, SLOTS * SHARD), 1.0, 6.0, ((0, 4), (1, 32)), jnp.float32)
    moment_one = normal_values(key_of[2], (GROUPS, SLOTS * SHARD), 3.0, 18.0, ((0, 4), (1, 32)), jnp.float32)
    moment_two = jnp.clip(jnp.exp(math.log(100.0) - 4.6051702 * jax.random.uniform(key_of[3], (GROUPS, SLOTS * SHARD), jnp.float32) ** shard_levels(key_of[3], (GROUPS, SLOTS * SHARD), ((0, 4), (1, 32)), -0.2, 0.2)), 1.0, 100.0)
    coding = draw_coding(jax.random.fold_in(key_of[6], 71), 0)
    holders = draw_holders(jax.random.fold_in(key_of[6], 71), 0)
    return {"grads": grads, "params": params, "moment_one": moment_one, "moment_two": moment_two, "coding": coding, "holders": holders}


def reference(grads, params, moment_one, moment_two, coding, holders):

    def add_partial(running_sum, partial_row):
        return (running_sum + partial_row.astype(jnp.float32), None)
    gradient, leftover = lax.scan(add_partial, jnp.zeros(grads.shape[1:], jnp.float32), grads)
    first_moment = 0.9 * moment_one + 0.1 * gradient
    second_moment = 0.95 * moment_two + 0.05 * gradient * gradient
    first_fix = 1.0 - 0.9 ** 10
    second_fix = 1.0 - 0.95 ** 10
    update = first_moment / first_fix / (jnp.sqrt(second_moment / second_fix) + 1e-08) + 0.1 * params
    new_params = params - 0.05 * update
    parity = jnp.einsum('gk,gn->kn', coding.astype(jnp.float32), new_params, precision=lax.Precision.HIGHEST)
    holder_cells = jnp.repeat(holders, SHARD, axis=0)
    group_numbers = jnp.arange(GROUPS, dtype=jnp.int32)
    parity_held = jnp.zeros_like(new_params)
    for parity_index in range(2):
        selection = (holder_cells[None, :, parity_index] == group_numbers[:, None]).astype(jnp.float32)
        parity_held = parity_held + selection * parity[parity_index][None, :]
    return (new_params, first_moment, second_moment, parity_held)
```

```python
import functools
import jax
import jax.numpy as jnp
from jax import lax
from jax.experimental import pallas as pl
from jax.experimental.pallas import tpu as pltpu
from jax.sharding import PartitionSpec as P

MESH = pl.DeviceIdType.MESH
LANES = 128
STEP = (2, 3, 1, 0)
FAR, BEFORE, AFTER, OWN = range(4)
PARTS = (((0, 1, 2), 0, 88), ((1, 2, 0), 88, 80), ((2, 0, 1), 168, 88))
ROWS = 256
ONE = {"far": (0, 1), "near": (1, 2), "own": (3, 1)}
UNITS = tuple(
    (ONE[a], ONE[b])
    for a, b in (
        ("far", "far"),
        ("far", "near"),
        ("near", "far"),
        ("near", "near"),
        ("far", "own"),
        ("own", "far"),
        ("own", "near"),
        ("near", "own"),
        ("own", "own"),
    )
)
UNITS2 = ((ONE["far"],), (ONE["near"],), (ONE["own"],))
UNITS3 = ((),)
STAGES = (UNITS, UNITS2, UNITS3)
LINK_COPIES = len(PARTS) * sum(len(u) for u in STAGES) * 6


def half(rows, unit):
    tiles = rows // 8
    return 8 * ((tiles + unit % 2) // 2)


def device(x, y, z, core):
    return {"group": y % 2 * 2 + core, "fsdp": y // 2 * 16 + x * 4 + z}


def kernel(grads, params, one, two, coding, holders, out_params, out_one, out_two, out_parity, *scratch):
    bufs = [scratch[8 * p : 8 * p + 8] for p in range(len(PARTS))]
    state, results, shared, link_send, link_recv, own_sem, peer_sem, peer_send, misc = scratch[8 * len(PARTS) :]
    group, fsdp = lax.axis_index("group"), lax.axis_index("fsdp")
    core = group % 2
    here = (fsdp // 4 % 4, fsdp // 16 * 2 + group // 2, fsdp % 4)

    def along(axis, distance):
        there = list(here)
        there[axis] = (there[axis] + distance) % 4
        return device(*there, core)

    ahead = [along(axis, 1) for axis in range(3)]
    behind = [along(axis, 3) for axis in range(3)]
    other_core = device(*here, 1 - core)
    partner = device(here[0], here[1] // 2 * 2 + 1 - here[1] % 2, here[2], core)

    places = [[(here[axis] + d) % 4 for d in STEP] for axis in range(3)]
    starts = (
        [v * (4 * ROWS) for v in places[0]],
        [v // 2 * (16 * ROWS) for v in places[1]],
        [v * ROWS for v in places[2]],
    )
    group_rows = [v % 2 * 2 for v in places[1]]

    def shard_of(p, slots, which):
        order, first, rows = PARTS[p]
        slot = {axis: slots[i] for i, axis in enumerate(order)}
        start = starts[0][slot[0]] + starts[1][slot[1]] + starts[2][slot[2]] + first
        return grads.at[pl.ds(pl.multiple_of(start, 8), rows), group_rows[slot[1]] + which]

    def slots_of(unit):
        out = [()]
        for first, count in unit:
            out = [s + (i,) for s in out for i in range(first, first + count)]
        return out

    def at(ref, lead, unit, rows=None):
        index = tuple(lead) + tuple(pl.ds(first, count) for first, count in unit)
        if rows is not None:
            index += (pl.ds(rows[0], rows[1] - rows[0]),)
        return ref.at[index] if index else ref

    def number(p, u, m):
        return (p * len(UNITS) + u) * 4 + m

    def load_own(p, u):
        for m in range(4):
            for s in slots_of(UNITS[u]):
                pltpu.make_async_copy(
                    shard_of(p, (m,) + s, core), bufs[p][0].at[(m,) + s], own_sem.at[number(p, u, m)]
                ).start()

    def give_peer(p, u, slots):
        for m in slots:
            for s in slots_of(UNITS[u]):
                pltpu.make_async_remote_copy(
                    src_ref=shard_of(p, (m,) + s, 1 - core),
                    dst_ref=bufs[p][1].at[(m,) + s],
                    send_sem=peer_send.at[p],
                    recv_sem=peer_sem.at[number(p, u, m)],
                    device_id=other_core,
                    device_id_type=MESH,
                ).start()

    def arrived(ref, sem):
        pltpu.make_async_copy(ref, ref, sem).wait()

    def ready(p, u, m):
        arrived(at(bufs[p][0], (m,), UNITS[u]), own_sem.at[number(p, u, m)])
        arrived(at(bufs[p][1], (m,), UNITS[u]), peer_sem.at[number(p, u, m)])

    def add(target, terms, slots):
        for s in slots:
            total = target.at[s][...] if s else target[...]
            for term in terms:
                total = total + (term.at[s][...] if s else term[...])
            if s:
                target.at[s][...] = total
            else:
                target[...] = total

    def local(unit):
        out = [()]
        for _, count in unit:
            out = [s + (i,) for s in out for i in range(count)]
        return out

    sent = []

    def link_number(p, stage, u, which):
        before = sum(len(units) for units in STAGES[:stage]) + u
        return (p * sum(len(units) for units in STAGES) + before) * 6 + which

    def send(p, stage, u, which, source, target, to):
        i = link_number(p, stage, u, which)
        copy = pltpu.make_async_remote_copy(
            src_ref=source,
            dst_ref=target,
            send_sem=link_send.at[i],
            recv_sem=link_recv.at[i],
            device_id=to,
            device_id_type=MESH,
        )
        copy.start()
        sent.append(copy)

    def came(p, stage, u, which, ref):
        arrived(ref, link_recv.at[link_number(p, stage, u, which)])

    def views(p, stage, u):
        order, _, rows = PARTS[p]
        unit = STAGES[stage][u]
        cut = half(rows, u)
        lead = (OWN,) * stage
        first, last = (0, cut), (cut, rows)
        values = lambda m, r=None: at(bufs[p][0], lead + (m,), unit, r)
        peers = lambda m, r=None: at(bufs[p][1], lead + (m,), unit, r)
        far = lambda way: at(bufs[p][2 + 2 * stage], (way,), unit, (0, cut if way == 0 else rows - cut))
        near = lambda way, r=None: at(bufs[p][3 + 2 * stage], (way,), unit, r)
        return order[stage], first, last, values, peers, far, near, local(unit)

    def send_far(p, stage, u):
        axis, first, last, values, peers, far, near, slots = views(p, stage, u)
        if stage == 0:
            ready(p, u, FAR)
            add(values(FAR), [peers(FAR)], slots)
        send(p, stage, u, 0, values(FAR, first), far(0), ahead[axis])
        send(p, stage, u, 1, values(FAR, last), far(1), behind[axis])

    def send_near(p, stage, u):
        axis, first, last, values, peers, far, near, slots = views(p, stage, u)
        if stage == 0:
            ready(p, u, AFTER)
            add(values(AFTER, last), [peers(AFTER, last)], slots)
        send(p, stage, u, 2, values(AFTER, last), near(0, last), ahead[axis])
        if stage == 0:
            ready(p, u, BEFORE)
            add(values(BEFORE, first), [peers(BEFORE, first)], slots)
        send(p, stage, u, 3, values(BEFORE, first), near(1, first), behind[axis])

    def pass_on(p, stage, u):
        axis, first, last, values, peers, far, near, slots = views(p, stage, u)
        came(p, stage, u, 0, far(0))
        add(values(AFTER, first), ([peers(AFTER, first)] if stage == 0 else []) + [far(0)], slots)
        send(p, stage, u, 4, values(AFTER, first), near(0, first), ahead[axis])
        came(p, stage, u, 1, far(1))
        add(values(BEFORE, last), ([peers(BEFORE, last)] if stage == 0 else []) + [far(1)], slots)
        send(p, stage, u, 5, values(BEFORE, last), near(1, last), behind[axis])

    def finish(p, stage, u):
        axis, first, last, values, peers, far, near, slots = views(p, stage, u)
        if stage == 0:
            ready(p, u, OWN)
        came(p, stage, u, 2, near(0, last))
        came(p, stage, u, 3, near(1, first))
        came(p, stage, u, 4, near(0, first))
        came(p, stage, u, 5, near(1, last))
        add(values(OWN), ([peers(OWN)] if stage == 0 else []) + [near(0), near(1)], slots)

    parts = range(len(PARTS))

    def every(step, *args):
        for p in parts:
            step(p, *args)

    def load(u):
        every(load_own, u - 1)

    def give(u):
        every(give_peer, u - 1, (FAR,))
        every(give_peer, u - 1, (AFTER, BEFORE))
        every(give_peer, u - 1, (OWN,))

    def begin(stage, u):
        every(send_far, stage, u - 1)
        every(send_near, stage, u - 1)

    def far_of(stage, u):
        every(send_far, stage, u - 1)

    def near_of(stage, u):
        every(send_near, stage, u - 1)

    def dep(stage, u):
        every(pass_on, stage, u - 1)

    def done(stage, u):
        every(finish, stage, u - 1)

    load(1)
    for i, ref in enumerate((params, one, two)):
        pltpu.make_async_copy(ref, state.at[i], misc.at[i]).start()
    load(2)
    barrier = pltpu.get_barrier_semaphore()
    for to in ahead + behind + [other_core]:
        pl.semaphore_signal(barrier, inc=1, device_id=to, device_id_type=MESH)
    pl.semaphore_wait(barrier, 7)
    give(1)
    give(2)
    begin(0, 1)
    load(3), give(3)
    begin(0, 2)
    load(4), give(4)
    dep(0, 1)
    begin(0, 3)
    load(5), give(5), load(6), give(6)
    dep(0, 2)
    done(0, 1), far_of(1, 1)
    begin(0, 4)
    load(7), give(7), load(8), give(8), load(9), give(9)
    dep(0, 3)
    done(0, 2), far_of(1, 2)
    begin(0, 5)
    done(0, 3), near_of(1, 1)
    dep(0, 4)
    begin(0, 6)
    done(0, 4), near_of(1, 2)
    dep(1, 1)
    dep(0, 5)
    begin(0, 7)
    done(0, 5), far_of(1, 3)
    dep(1, 2)
    dep(0, 6)
    begin(0, 8)
    done(0, 6), done(1, 1), far_of(2, 1)
    dep(0, 7)
    begin(0, 9)
    done(0, 7), done(1, 2), near_of(2, 1)
    dep(0, 8), dep(0, 9)
    done(0, 8), near_of(1, 3)
    dep(2, 1), dep(1, 3)

    for i in range(3):
        arrived(state.at[i], misc.at[i])
    for p in parts:
        arrived(bufs[p][0], peer_send.at[p])

    copies, across, beside = [], [], []
    for p in parts:
        finish(p, 0, 8)
        finish(p, 1, 2)
        finish(p, 2, 0)
        _, start, rows = PARTS[p]
        mine = pl.ds(start, rows)
        gradient = bufs[p][0].at[OWN, OWN, OWN][...]
        values = state.at[0, mine][...]
        first_moment = 0.9 * state.at[1, mine][...] + 0.1 * gradient
        second_moment = 0.95 * state.at[2, mine][...] + 0.05 * gradient * gradient
        first_fix = 1.0 - 0.9**10
        second_fix = 1.0 - 0.95**10
        update = first_moment / first_fix / (jnp.sqrt(second_moment / second_fix) + 1e-08) + 0.1 * values
        shared.at[0, mine][...] = values - 0.05 * update
        results.at[0, mine][...] = first_moment
        results.at[1, mine][...] = second_moment
        for n, (to, slot, kept) in enumerate(((partner, 2, across), (other_core, 1, beside))):
            copy = pltpu.make_async_remote_copy(
                src_ref=shared.at[0, mine],
                dst_ref=shared.at[slot, mine],
                send_sem=misc.at[3 + 6 * p + 2 * n],
                recv_sem=misc.at[4 + 6 * p + 2 * n],
                device_id=to,
                device_id_type=MESH,
            )
            copy.start()
            kept.append(copy)
        for n, (source, target) in enumerate(
            ((shared.at[0], out_params), (results.at[0], out_one), (results.at[1], out_two))
        ):
            copy = pltpu.make_async_copy(source.at[mine], target.at[mine], misc.at[21 + 4 * p + n])
            copy.start()
            copies.append(copy)

    for copy in sent:
        copy.wait_send()

    def weight(g):
        none = jnp.float32(0.0)
        return jnp.where(holders[0, 0] == group, coding[0, g], none) + jnp.where(
            holders[0, 1] == group, coding[1, g], none
        )

    far_side = (1 - group // 2) * 2
    weights = [
        weight(group),
        weight(group // 2 * 2 + 1 - core),
        weight(far_side + core),
        weight(far_side + 1 - core),
    ]
    relays = []
    for p in parts:
        _, start, rows = PARTS[p]
        mine = pl.ds(start, rows)
        across[p].wait()
        copy = pltpu.make_async_remote_copy(
            src_ref=shared.at[2, mine],
            dst_ref=shared.at[3, mine],
            send_sem=misc.at[7 + 6 * p],
            recv_sem=misc.at[8 + 6 * p],
            device_id=other_core,
            device_id_type=MESH,
        )
        copy.start()
        relays.append(copy)
    for p in parts:
        _, start, rows = PARTS[p]
        mine = pl.ds(start, rows)
        beside[p].wait()
        relays[p].wait()
        total = weights[0] * shared.at[0, mine][...]
        for slot in range(1, 4):
            total = total + weights[slot] * shared.at[slot, mine][...]
        results.at[2, mine][...] = total
        copy = pltpu.make_async_copy(results.at[2, mine], out_parity.at[mine], misc.at[24 + 4 * p])
        copy.start()
        copies.append(copy)
    for copy in copies:
        copy.wait()


def shards(grads, params, moment_one, moment_two, coding, holders):
    rows = grads.shape[2] // LANES
    partial = grads.reshape(4, rows, LANES).transpose(1, 0, 2)
    flat = lambda t: t.reshape(ROWS, LANES)
    anywhere = pl.BlockSpec(memory_space=pltpu.HBM)
    scalars = pl.BlockSpec(memory_space=pltpu.SMEM)
    f32 = jnp.float32
    scratch = []
    for _, _, n in PARTS:
        h = max(half(n, 0), half(n, 1), n - half(n, 0))
        scratch += [
            pltpu.VMEM((4, 4, 4, n, LANES), f32),
            pltpu.VMEM((4, 4, 4, n, LANES), f32),
            pltpu.VMEM((2, 4, 4, h, LANES), f32),
            pltpu.VMEM((2, 4, 4, n, LANES), f32),
            pltpu.VMEM((2, 4, h, LANES), f32),
            pltpu.VMEM((2, 4, n, LANES), f32),
            pltpu.VMEM((2, h, LANES), f32),
            pltpu.VMEM((2, n, LANES), f32),
        ]
    scratch += [
        pltpu.VMEM((3, ROWS, LANES), f32),
        pltpu.VMEM((3, ROWS, LANES), f32),
        pltpu.VMEM((4, ROWS, LANES), f32),
        pltpu.SemaphoreType.DMA((LINK_COPIES,)),
        pltpu.SemaphoreType.DMA((LINK_COPIES,)),
        pltpu.SemaphoreType.DMA((len(PARTS) * len(UNITS) * 4,)),
        pltpu.SemaphoreType.DMA((len(PARTS) * len(UNITS) * 4,)),
        pltpu.SemaphoreType.DMA((len(PARTS),)),
        pltpu.SemaphoreType.DMA((3 + 10 * len(PARTS),)),
    ]
    out = pl.pallas_call(
        kernel,
        out_shape=[jax.ShapeDtypeStruct((ROWS, LANES), f32)] * 4,
        in_specs=[anywhere] * 4 + [scalars] * 2,
        out_specs=[anywhere] * 4,
        scratch_shapes=scratch,
        compiler_params=pltpu.CompilerParams(
            collective_id=0, has_side_effects=True, vmem_limit_bytes=60 * 1024 * 1024
        ),
    )(partial, flat(params), flat(moment_one), flat(moment_two), coding.T, holders)
    return tuple(t.reshape(1, ROWS * LANES) for t in out)


def solution(mesh):
    return jax.shard_map(
        shards,
        mesh=mesh,
        in_specs=(
            P(("group", "fsdp"), None, None),
            P("group", "fsdp"),
            P("group", "fsdp"),
            P("group", "fsdp"),
            P(),
            P("fsdp", None),
        ),
        out_specs=(P("group", "fsdp"), P("group", "fsdp"), P("group", "fsdp"), P("group", "fsdp")),
        check_vma=False,
    )
```

```python
import functools
import jax
import jax.numpy as jnp
from jax import lax
from jax.experimental import pallas as pl
from jax.experimental.pallas import tpu as pltpu
from jax.sharding import PartitionSpec as P

MESH = pl.DeviceIdType.MESH
LANES = 128
STEP = (2, 3, 1, 0)
FAR, BEFORE, AFTER, OWN = range(4)
PARTS = (((0, 1, 2), 0, 88), ((1, 2, 0), 88, 80), ((2, 0, 1), 168, 88))
ROWS = 256
ONE = {"far": (0, 1), "near": (1, 2), "own": (3, 1)}
UNITS = tuple(
    (ONE[a], ONE[b])
    for a, b in (
        ("far", "far"),
        ("far", "near"),
        ("near", "far"),
        ("near", "near"),
        ("far", "own"),
        ("own", "far"),
        ("own", "near"),
        ("near", "own"),
        ("own", "own"),
    )
)
UNITS2 = ((ONE["far"],), (ONE["near"],), (ONE["own"],))
UNITS3 = ((),)
STAGES = (UNITS, UNITS2, UNITS3)
PER_PART = sum(len(units) for units in STAGES)
LOADS = (((0, 1), (0, 1)), ((0, 1), (1, 3)), ((1, 2), (0, 4)), ((3, 1), (0, 4)))
LOAD_OF = (0, 1, 2, 2, 1, 3, 3, 2, 3)
PLAN = (
    "g1 g2 g3 b1",
    "G1 g4 b2 G2",
    "g5 g6 b3 G3",
    "d1 g7 g8 b4",
    "g9 G4 d2 o1",
    "F1 b5 d3 o2",
    "F2 b6 d4 o3",
    "N1 b7 d5 D1",
    "o4 N2 b8 d6",
    "o5 F3 b9 d7",
    "D2 o6 O1 f1",
    "d8 o7 O2 n1",
    "d9 o8 N3 e1",
    "D3",
)


def half(rows, unit):
    tiles = rows // 8
    return 8 * ((tiles + unit % 2) // 2)


def device(x, y, z, core):
    return {"group": y % 2 * 2 + core, "fsdp": y // 2 * 16 + x * 4 + z}


def kernel(grads, params, one, two, coding, holders, results, *scratch):
    bufs = [scratch[8 * p : 8 * p + 8] for p in range(len(PARTS))]
    state, shared, link_send, link_recv, own_sem, peer_sem, peer_send, misc = scratch[8 * len(PARTS) :]
    group, fsdp = lax.axis_index("group"), lax.axis_index("fsdp")
    core = group % 2
    here = (fsdp // 4 % 4, fsdp // 16 * 2 + group // 2, fsdp % 4)

    def along(axis, distance):
        there = list(here)
        there[axis] = (there[axis] + distance) % 4
        return device(*there, core)

    ahead = [along(axis, 1) for axis in range(3)]
    behind = [along(axis, 3) for axis in range(3)]
    other_core = device(*here, 1 - core)
    partner = device(here[0], here[1] // 2 * 2 + 1 - here[1] % 2, here[2], core)

    places = [[(here[axis] + d) % 4 for d in STEP] for axis in range(3)]
    starts = (
        [v * (4 * ROWS) for v in places[0]],
        [v // 2 * (16 * ROWS) for v in places[1]],
        [v * ROWS for v in places[2]],
    )
    group_rows = [v % 2 * 2 for v in places[1]]

    def shard_of(p, slots, which):
        order, first, rows = PARTS[p]
        slot = {axis: slots[i] for i, axis in enumerate(order)}
        start = starts[0][slot[0]] + starts[1][slot[1]] + starts[2][slot[2]] + first
        return grads.at[pl.ds(pl.multiple_of(start, 8), rows), group_rows[slot[1]] + which]

    def slots_of(unit):
        out = [()]
        for first, count in unit:
            out = [s + (i,) for s in out for i in range(first, first + count)]
        return out

    def at(ref, lead, unit, rows=None):
        index = tuple(lead) + tuple(pl.ds(first, count) for first, count in unit)
        if rows is not None:
            index += (pl.ds(rows[0], rows[1] - rows[0]),)
        return ref.at[index] if index else ref

    def load_own(p, g):
        for m in range(4):
            for s in slots_of(LOADS[g]):
                pltpu.make_async_copy(
                    shard_of(p, (m,) + s, core), bufs[p][0].at[(m,) + s], own_sem.at[p * len(LOADS) + g]
                ).start()

    def give_peer(p, block, slots, sem):
        for m in slots:
            for s in slots_of(block):
                pltpu.make_async_remote_copy(
                    src_ref=shard_of(p, (m,) + s, 1 - core),
                    dst_ref=bufs[p][1].at[(m,) + s],
                    send_sem=peer_send.at[p],
                    recv_sem=sem,
                    device_id=other_core,
                    device_id_type=MESH,
                ).start()

    def sent_on(p, u):
        return peer_sem.at[p * len(UNITS) + u]

    def kept(p, g):
        return peer_sem.at[(len(PARTS) * len(UNITS)) + p * len(LOADS) + g]

    def arrived(ref, sem):
        pltpu.make_async_copy(ref, ref, sem).wait()

    waited = set()

    def ready(p, u, m):
        g, rest = LOAD_OF[u], m == OWN
        if (p, g) not in waited:
            waited.add((p, g))
            arrived(at(bufs[p][0], (), ((0, 4),) + LOADS[g]), own_sem.at[p * len(LOADS) + g])
        if rest and (p, g, OWN) not in waited:
            waited.add((p, g, OWN))
            arrived(at(bufs[p][1], (OWN,), LOADS[g]), kept(p, g))
        if not rest and (p, u, FAR) not in waited:
            waited.add((p, u, FAR))
            arrived(at(bufs[p][1], (), ((0, 3),) + UNITS[u]), sent_on(p, u))

    def add(target, terms, slots):
        for s in slots:
            total = target.at[s][...] if s else target[...]
            for term in terms:
                total = total + (term.at[s][...] if s else term[...])
            if s:
                target.at[s][...] = total
            else:
                target[...] = total

    def local(unit):
        out = [()]
        for _, count in unit:
            out = [s + (i,) for s in out for i in range(count)]
        return out

    def landing(p, stage, u, kind):
        return link_recv.at[(p * PER_PART + sum(len(units) for units in STAGES[:stage]) + u) * 3 + kind]

    def send(p, stage, u, kind, source, target, to):
        pltpu.make_async_remote_copy(
            src_ref=source,
            dst_ref=target,
            send_sem=link_send.at[3 * p + stage],
            recv_sem=landing(p, stage, u, kind),
            device_id=to,
            device_id_type=MESH,
        ).start()

    def views(p, stage, u):
        order, _, rows = PARTS[p]
        unit = STAGES[stage][u]
        cut = half(rows, u)
        lead = (OWN,) * stage
        first, last = (0, cut), (cut, rows)
        values = lambda m, r=None: at(bufs[p][0], lead + (m,), unit, r)
        peers = lambda m, r=None: at(bufs[p][1], lead + (m,), unit, r)
        far = lambda way: at(bufs[p][2 + 2 * stage], (way,), unit, (0, cut if way == 0 else rows - cut))
        near = lambda way, r=None: at(bufs[p][3 + 2 * stage], (way,), unit, r)
        return order[stage], first, last, values, peers, far, near, local(unit)

    def send_far(p, stage, u):
        axis, first, last, values, peers, far, near, slots = views(p, stage, u)
        if stage == 0:
            ready(p, u, FAR)
            add(values(FAR), [peers(FAR)], slots)
        send(p, stage, u, 0, values(FAR, first), far(0), ahead[axis])
        send(p, stage, u, 1, values(FAR, last), far(1), behind[axis])

    def send_near(p, stage, u):
        axis, first, last, values, peers, far, near, slots = views(p, stage, u)
        if stage == 0:
            ready(p, u, AFTER)
            add(values(AFTER, last), [peers(AFTER, last)], slots)
        send(p, stage, u, 2, values(AFTER, last), near(0, last), ahead[axis])
        if stage == 0:
            ready(p, u, BEFORE)
            add(values(BEFORE, first), [peers(BEFORE, first)], slots)
        send(p, stage, u, 2, values(BEFORE, first), near(1, first), behind[axis])

    def pass_on(p, stage, u):
        axis, first, last, values, peers, far, near, slots = views(p, stage, u)
        arrived(far(0), landing(p, stage, u, 0))
        add(values(AFTER, first), ([peers(AFTER, first)] if stage == 0 else []) + [far(0)], slots)
        send(p, stage, u, 2, values(AFTER, first), near(0, first), ahead[axis])
        arrived(far(1), landing(p, stage, u, 1))
        add(values(BEFORE, last), ([peers(BEFORE, last)] if stage == 0 else []) + [far(1)], slots)
        send(p, stage, u, 2, values(BEFORE, last), near(1, last), behind[axis])

    def finish(p, stage, u):
        axis, first, last, values, peers, far, near, slots = views(p, stage, u)
        if stage == 0:
            ready(p, u, OWN)
        arrived(at(bufs[p][3 + 2 * stage], (), ((0, 2),) + STAGES[stage][u]), landing(p, stage, u, 2))
        add(values(OWN), ([peers(OWN)] if stage == 0 else []) + [near(0), near(1)], slots)

    parts = range(len(PARTS))

    def every(step, *args):
        for p in parts:
            step(p, *args)

    def load(g):
        every(load_own, g - 1)

    def give(u):
        for p in parts:
            give_peer(p, UNITS[u - 1], (FAR, AFTER, BEFORE), sent_on(p, u - 1))

    def give_own(g):
        for p in parts:
            give_peer(p, LOADS[g - 1], (OWN,), kept(p, g - 1))

    def begin(u):
        every(send_far, 0, u - 1)
        every(send_near, 0, u - 1)

    steps = {
        "g": give,
        "G": give_own,
        "b": begin,
        "d": lambda u: every(pass_on, 0, u - 1),
        "o": lambda u: every(finish, 0, u - 1),
        "F": lambda u: every(send_far, 1, u - 1),
        "N": lambda u: every(send_near, 1, u - 1),
        "D": lambda u: every(pass_on, 1, u - 1),
        "O": lambda u: every(finish, 1, u - 1),
        "f": lambda u: every(send_far, 2, u - 1),
        "n": lambda u: every(send_near, 2, u - 1),
        "e": lambda u: every(pass_on, 2, u - 1),
    }

    load(1)
    load(2)
    for i, ref in enumerate((params, one, two)):
        pltpu.make_async_copy(ref, state.at[i], misc.at[i]).start()
    load(3)
    load(4)
    barrier = pltpu.get_barrier_semaphore()
    for to in ahead + behind + [other_core]:
        pl.semaphore_signal(barrier, inc=1, device_id=to, device_id_type=MESH)
    pl.semaphore_wait(barrier, 7)
    for step in " ".join(PLAN).split():
        steps[step[0]](int(step[1]))

    for i in range(3):
        arrived(state.at[i], misc.at[i])
    for p in parts:
        arrived(bufs[p][0], peer_send.at[p])

    across, beside = [], []
    for p in parts:
        finish(p, 0, 8)
        finish(p, 1, 2)
        finish(p, 2, 0)
        _, start, rows = PARTS[p]
        mine = pl.ds(start, rows)
        gradient = bufs[p][0].at[OWN, OWN, OWN][...]
        values = state.at[0, mine][...]
        first_moment = 0.9 * state.at[1, mine][...] + 0.1 * gradient
        second_moment = 0.95 * state.at[2, mine][...] + 0.05 * gradient * gradient
        first_fix = 1.0 - 0.9**10
        second_fix = 1.0 - 0.95**10
        update = first_moment / first_fix / (jnp.sqrt(second_moment / second_fix) + 1e-08) + 0.1 * values
        new_params = values - 0.05 * update
        shared.at[0, mine][...] = new_params
        results.at[0, mine][...] = new_params
        results.at[1, mine][...] = first_moment
        results.at[2, mine][...] = second_moment
        for n, (to, slot, kept) in enumerate(((partner, 2, across), (other_core, 1, beside))):
            copy = pltpu.make_async_remote_copy(
                src_ref=shared.at[0, mine],
                dst_ref=shared.at[slot, mine],
                send_sem=misc.at[3 + 6 * p + 2 * n],
                recv_sem=misc.at[4 + 6 * p + 2 * n],
                device_id=to,
                device_id_type=MESH,
            )
            copy.start()
            kept.append(copy)

    for p in parts:
        for stage in range(3):
            ref = at(bufs[p][0], (), ((0, 3),)) if stage == 0 else bufs[p][0].at[(pl.ds(0, 3),) + (0,) * stage]
            arrived(ref, link_send.at[3 * p + stage])

    def weight(g):
        none = jnp.float32(0.0)
        return jnp.where(holders[0, 0] == group, coding[0, g], none) + jnp.where(
            holders[0, 1] == group, coding[1, g], none
        )

    far_side = (1 - group // 2) * 2
    weights = [
        weight(group),
        weight(group // 2 * 2 + 1 - core),
        weight(far_side + core),
        weight(far_side + 1 - core),
    ]
    relays = []
    for p in parts:
        _, start, rows = PARTS[p]
        mine = pl.ds(start, rows)
        across[p].wait()
        copy = pltpu.make_async_remote_copy(
            src_ref=shared.at[2, mine],
            dst_ref=shared.at[3, mine],
            send_sem=misc.at[7 + 6 * p],
            recv_sem=misc.at[8 + 6 * p],
            device_id=other_core,
            device_id_type=MESH,
        )
        copy.start()
        relays.append(copy)
    for p in parts:
        _, start, rows = PARTS[p]
        mine = pl.ds(start, rows)
        beside[p].wait()
        relays[p].wait()
        total = weights[0] * shared.at[0, mine][...]
        for slot in range(1, 4):
            total = total + weights[slot] * shared.at[slot, mine][...]
        results.at[3, mine][...] = total


def write(results, *rest):
    outs, sems = rest[:-1], rest[-1]
    copies = [pltpu.make_async_copy(results.at[i], out, sems.at[i]) for i, out in enumerate(outs)]
    for copy in copies:
        copy.start()
    for copy in copies:
        copy.wait()


def shards(grads, params, moment_one, moment_two, coding, holders):
    rows = grads.shape[2] // LANES
    partial = grads.reshape(4, rows, LANES).transpose(1, 0, 2)
    flat = lambda t: t.reshape(ROWS, LANES)
    anywhere = pl.BlockSpec(memory_space=pltpu.HBM)
    scalars = pl.BlockSpec(memory_space=pltpu.SMEM)
    f32 = jnp.float32
    scratch = []
    for _, _, n in PARTS:
        h = max(half(n, 0), half(n, 1), n - half(n, 0))
        scratch += [
            pltpu.VMEM((4, 4, 4, n, LANES), f32),
            pltpu.VMEM((4, 4, 4, n, LANES), f32),
            pltpu.VMEM((2, 4, 4, h, LANES), f32),
            pltpu.VMEM((2, 4, 4, n, LANES), f32),
            pltpu.VMEM((2, 4, h, LANES), f32),
            pltpu.VMEM((2, 4, n, LANES), f32),
            pltpu.VMEM((2, h, LANES), f32),
            pltpu.VMEM((2, n, LANES), f32),
        ]
    scratch += [
        pltpu.VMEM((3, ROWS, LANES), f32),
        pltpu.VMEM((4, ROWS, LANES), f32),
        pltpu.SemaphoreType.DMA((len(PARTS) * 3,)),
        pltpu.SemaphoreType.DMA((len(PARTS) * PER_PART * 3,)),
        pltpu.SemaphoreType.DMA((len(PARTS) * len(LOADS),)),
        pltpu.SemaphoreType.DMA((len(PARTS) * (len(UNITS) + len(LOADS)),)),
        pltpu.SemaphoreType.DMA((len(PARTS),)),
        pltpu.SemaphoreType.DMA((3 + 6 * len(PARTS),)),
    ]
    vmem = pl.BlockSpec(memory_space=pltpu.VMEM)
    results = pl.pallas_call(
        kernel,
        out_shape=pltpu.VMEM((4, ROWS, LANES), f32),
        in_specs=[anywhere] * 4 + [scalars] * 2,
        out_specs=vmem,
        scratch_shapes=scratch,
        compiler_params=pltpu.CompilerParams(
            collective_id=0, has_side_effects=True, vmem_limit_bytes=56 * 1024 * 1024
        ),
    )(partial, flat(params), flat(moment_one), flat(moment_two), coding.T, holders)
    out = pl.pallas_call(
        write,
        out_shape=[jax.ShapeDtypeStruct((ROWS, LANES), f32)] * 4,
        in_specs=[vmem],
        out_specs=[anywhere] * 4,
        scratch_shapes=[pltpu.SemaphoreType.DMA((4,))],
    )(results)
    return tuple(t.reshape(1, ROWS * LANES) for t in out)


def solution(mesh):
    return jax.shard_map(
        shards,
        mesh=mesh,
        in_specs=(
            P(("group", "fsdp"), None, None),
            P("group", "fsdp"),
            P("group", "fsdp"),
            P("group", "fsdp"),
            P(),
            P("fsdp", None),
        ),
        out_specs=(P("group", "fsdp"), P("group", "fsdp"), P("group", "fsdp"), P("group", "fsdp")),
        check_vma=False,
    )
```

```python
import jax
import jax.numpy as jnp
from jax import lax
from jax.experimental import pallas as pl
from jax.experimental.pallas import tpu as pltpu
from jax.sharding import PartitionSpec as P

MESH = pl.DeviceIdType.MESH
LANES = 128
ROWS = 256
STEP = (2, 3, 1, 0)
FAR, BEFORE, AFTER, OWN = range(4)
ORDERS = ((0, 1, 2), (1, 2, 0), (2, 0, 1))
CHUNKS = ((0, (64, 64, 64)), (192, (24, 16, 24)))
ONE = {"far": (0, 1), "near": (1, 2), "own": (3, 1)}
UNITS = tuple(
    (ONE[a], ONE[b])
    for a, b in (
        ("far", "far"),
        ("far", "near"),
        ("near", "far"),
        ("near", "near"),
        ("far", "own"),
        ("own", "far"),
        ("own", "near"),
        ("near", "own"),
        ("own", "own"),
    )
)
STAGES = (UNITS, ((ONE["far"],), (ONE["near"],), (ONE["own"],)), ((),))
PER_CHUNK = sum(len(units) for units in STAGES)
LOADS = (((0, 1), (0, 1)), ((0, 1), (1, 3)), ((1, 2), (0, 4)), ((3, 1), (0, 4)))
LOAD_OF = (0, 1, 2, 2, 1, 3, 3, 2, 3)
PIECE = 64
GIVEN = 2 * len(UNITS) + len(LOADS)
PLAN = (
    "0g2 0g4 0h2 1g1",
    "0h4 0G2 0b2 0g1",
    "1h1 0G3 0b4 1l1",
    "1l2 1l3 0g3 1l4",
    "0h1 0c2 1b1 1G1",
    "1g2 0h3 0c4 0G1",
    "0b1 0g6 1h2 1c1",
    "1g3 0h6 0d2 1G2",
    "0g5 1h3 0G4 0b3",
    "1g5 0h5 0c1 0d4",
    "1G3 0g7 1h5 1g6",
    "1d1 0h7 1g4 1b2",
    "1h6 0g8 0c3 1h4",
    "1G4 0b6 1g8 0d1",
    "0h8 1c2 1g7 1h8",
    "0o2 0F2 0g9 1h7",
    "1g9 0h9 0d3 1h9",
    "1b3 0c6 0b5 1c3",
    "0o4 0N2 1o1 1F1",
    "1d2 1b5 0c5 0d6",
    "0o1 0F1 0b7 0D2",
    "0o3 0N1 1d3 0d5",
    "1c5 1b6 0c7 1o2",
    "1F2 1d5 1b4 0o6",
    "1c6 0b8 0D1 0d7",
    "1c4 1o3 1N1 1D1",
    "1b8 0o5 0F3 1d6",
    "0c8 1o5 1F3 1b7",
    "1c8 1d4 0b9 0d8",
    "0O1 0f1 0o7 0O2",
    "0n1 1c7 1b9 0c9",
    "1d8 1o6 1O1 1f1",
    "1c9 1d7 1o4 1N2",
    "1D2 0d9 0o8 0N3",
    "0D3 0e1 1d9 1o8",
    "1N3 1D3 1o7 1O2",
    "1n1 1e1 0q1 1q1",
    "0r1 1r1 0t1 1t1",
)


def device(x, y, z, core):
    return {"group": y % 2 * 2 + core, "fsdp": y // 2 * 16 + x * 4 + z}


def kernel(grads, params, one, two, coding, holders, results, *scratch):
    bufs = [scratch[8 * k : 8 * k + 8] for k in range(len(CHUNKS))]
    state, shared, codes, held, link_send, link_recv, own_sem, peer_sem, peer_send, misc = scratch[8 * len(CHUNKS) :]
    group, fsdp = lax.axis_index("group"), lax.axis_index("fsdp")
    core = group % 2
    here = (fsdp // 4 % 4, fsdp // 16 * 2 + group // 2, fsdp % 4)

    def along(axis, distance):
        there = list(here)
        there[axis] = (there[axis] + distance) % 4
        return device(*there, core)

    ahead = [along(axis, 1) for axis in range(3)]
    behind = [along(axis, 3) for axis in range(3)]
    other_core = device(*here, 1 - core)
    partner = device(here[0], here[1] // 2 * 2 + 1 - here[1] % 2, here[2], core)

    places = [[(here[axis] + d) % 4 for d in STEP] for axis in range(3)]
    starts = (
        [v * (4 * ROWS) for v in places[0]],
        [v // 2 * (16 * ROWS) for v in places[1]],
        [v * ROWS for v in places[2]],
    )
    group_rows = [v % 2 * 2 for v in places[1]]

    def parts_of(k, odd=0):
        first, sizes = CHUNKS[k]
        out, at_row = [], 0
        for order, rows in zip(ORDERS, sizes):
            cut = 8 * ((rows // 8 + odd) // 2)
            out.append((order, at_row, at_row + cut, at_row + rows, first + at_row))
            at_row += rows
        return out

    def slots_of(unit):
        out = [()]
        for first, count in unit:
            out = [s + (i,) for s in out for i in range(first, first + count)]
        return out

    def at(ref, lead, unit, rows=None):
        index = tuple(lead) + tuple(pl.ds(first, count) for first, count in unit)
        if rows is not None:
            index += (pl.ds(rows[0], rows[1] - rows[0]),)
        return ref.at[index] if index else ref

    def arrived(ref, sem):
        pltpu.make_async_copy(ref, ref, sem).wait()

    def terms(k, slots, which):
        for order, low, _, high, first in parts_of(k):
            slot = {axis: slots[i] for i, axis in enumerate(order)}
            start = starts[0][slot[0]] + starts[1][slot[1]] + starts[2][slot[2]] + first
            rows = pl.ds(pl.multiple_of(start, 8), high - low)
            yield grads.at[rows, group_rows[slot[1]] + which], slots + (pl.ds(low, high - low),)

    def load(k, g):
        for m in range(4):
            for s in slots_of(LOADS[g]):
                for source, place in terms(k, (m,) + s, core):
                    pltpu.make_async_copy(source, bufs[k][0].at[place], own_sem.at[k * len(LOADS) + g]).start()

    def give_peer(k, block, slots, sem):
        for m in slots:
            for s in slots_of(block):
                for source, place in terms(k, (m,) + s, 1 - core):
                    pltpu.make_async_remote_copy(
                        src_ref=source,
                        dst_ref=bufs[k][1].at[place],
                        send_sem=peer_send.at[k],
                        recv_sem=sem,
                        device_id=other_core,
                        device_id_type=MESH,
                    ).start()

    def given(k, kind, i):
        return peer_sem.at[k * GIVEN + kind * len(UNITS) + i]

    waited = set()

    def ready(k, u, kind):
        g = LOAD_OF[u]
        if (k, g) not in waited:
            waited.add((k, g))
            arrived(at(bufs[k][0], (), ((0, 4),) + LOADS[g]), own_sem.at[k * len(LOADS) + g])
        if kind < 2:
            slots = ((0, 1), (1, 2))[kind]
            arrived(at(bufs[k][1], (), (slots,) + UNITS[u]), given(k, kind, u))
        elif (k, g, OWN) not in waited:
            waited.add((k, g, OWN))
            arrived(at(bufs[k][1], (OWN,), LOADS[g]), given(k, 2, g))

    def add(refs):
        total = refs[0][...]
        for ref in refs[1:]:
            total = total + ref[...]
        refs[0][...] = total

    def landing(k, stage, u, kind):
        return link_recv.at[(k * PER_CHUNK + sum(len(units) for units in STAGES[:stage]) + u) * 2 + kind]

    def send(k, stage, u, kind, source, target, to):
        pltpu.make_async_remote_copy(
            src_ref=source,
            dst_ref=target,
            send_sem=link_send.at[3 * k + stage],
            recv_sem=landing(k, stage, u, kind),
            device_id=to,
            device_id_type=MESH,
        ).start()

    def values(k, stage, u, slot, rows):
        return at(bufs[k][0], (OWN,) * stage + (slot,), STAGES[stage][u], rows)

    def far(k, stage, u, rows=None):
        return at(bufs[k][2 + 2 * stage], (), STAGES[stage][u], rows)

    def near(k, stage, u, way, rows=None):
        return at(bufs[k][3 + 2 * stage], (way,), STAGES[stage][u], rows)

    def sum_up(k, stage, u, slot, rows, others):
        lead = (OWN,) * stage + (slot,)
        here_rows = (pl.ds(rows[0], rows[1] - rows[0]),)
        for s in slots_of(STAGES[stage][u]):
            refs = [bufs[k][0].at[lead + s + here_rows]]
            if stage == 0:
                refs.append(bufs[k][1].at[lead + s + here_rows])
            refs += [ref.at[extra + s + here_rows] for ref, extra in others]
            if len(refs) > 1:
                add(refs)

    def send_far(k, stage, u):
        whole = (0, sum(CHUNKS[k][1]))
        if stage == 0:
            ready(k, u, 0)
        sum_up(k, stage, u, FAR, whole, [])
        for order, low, cut, high, _ in parts_of(k, u % 2):
            axis = order[stage]
            for rows, to in (((low, cut), ahead[axis]), ((cut, high), behind[axis])):
                send(k, stage, u, 0, values(k, stage, u, FAR, rows), far(k, stage, u, rows), to)

    def send_near(k, stage, u):
        if stage == 0:
            ready(k, u, 1)
        for order, low, cut, high, _ in parts_of(k, u % 2):
            axis = order[stage]
            for slot, way, rows, to in ((AFTER, 0, (cut, high), ahead[axis]), (BEFORE, 1, (low, cut), behind[axis])):
                sum_up(k, stage, u, slot, rows, [])
                send(k, stage, u, 1, values(k, stage, u, slot, rows), near(k, stage, u, way, rows), to)

    def pass_on(k, stage, u):
        arrived(far(k, stage, u), landing(k, stage, u, 0))
        for order, low, cut, high, _ in parts_of(k, u % 2):
            axis = order[stage]
            for slot, way, rows, to in ((AFTER, 0, (low, cut), ahead[axis]), (BEFORE, 1, (cut, high), behind[axis])):
                sum_up(k, stage, u, slot, rows, [(bufs[k][2 + 2 * stage], ())])
                send(k, stage, u, 1, values(k, stage, u, slot, rows), near(k, stage, u, way, rows), to)

    def finish(k, stage, u):
        if stage == 0:
            ready(k, u, 2)
        arrived(at(bufs[k][3 + 2 * stage], (), ((0, 2),) + STAGES[stage][u]), landing(k, stage, u, 1))
        landed = bufs[k][3 + 2 * stage]
        sum_up(k, stage, u, OWN, (0, sum(CHUNKS[k][1])), [(landed, (0,)), (landed, (1,))])

    def pieces(k):
        first, rows = CHUNKS[k][0], sum(CHUNKS[k][1])
        return [(first + at_row, first // PIECE + i) for i, at_row in enumerate(range(0, rows, PIECE))]

    def share(piece, source, target, to, n):
        start, number = piece
        mine = pl.ds(start, PIECE)
        copy = pltpu.make_async_remote_copy(
            src_ref=shared.at[source, mine],
            dst_ref=shared.at[target, mine],
            send_sem=misc.at[5 + 6 * number + 2 * n],
            recv_sem=misc.at[6 + 6 * number + 2 * n],
            device_id=to,
            device_id_type=MESH,
        )
        copy.start()
        return copy

    shares = {}

    def step_params(k, _):
        finish(k, 0, 8)
        finish(k, 1, 2)
        finish(k, 2, 0)
        if "state" not in waited:
            waited.add("state")
            for i in range(3):
                arrived(state.at[i], misc.at[i])
        for piece in pieces(k):
            mine = pl.ds(piece[0], PIECE)
            gradient = bufs[k][0].at[OWN, OWN, OWN, pl.ds(piece[0] - CHUNKS[k][0], PIECE)][...]
            values = state.at[0, mine][...]
            first_moment = 0.9 * state.at[1, mine][...] + 0.1 * gradient
            second_moment = 0.95 * state.at[2, mine][...] + 0.05 * gradient * gradient
            first_fix = 1.0 - 0.9**10
            second_fix = 1.0 - 0.95**10
            update = first_moment / first_fix / (jnp.sqrt(second_moment / second_fix) + 1e-08) + 0.1 * values
            new_params = values - 0.05 * update
            shared.at[0, mine][...] = new_params
            shares[piece] = [share(piece, 0, 2, partner, 0), share(piece, 0, 1, other_core, 1)]
            results.at[0, mine][...] = new_params
            results.at[1, mine][...] = first_moment
            results.at[2, mine][...] = second_moment

    def relay(k, _):
        for piece in pieces(k):
            shares[piece][0].wait()
            shares[piece].append(share(piece, 2, 3, other_core, 2))

    def weight(g):
        none = jnp.float32(0.0)
        return jnp.where(held[0, 0] == group, codes[0, g], none) + jnp.where(held[0, 1] == group, codes[1, g], none)

    far_side = (1 - group // 2) * 2
    def weights():
        arrived(codes, misc.at[3])
        arrived(held, misc.at[4])
        return [
            weight(group),
            weight(group // 2 * 2 + 1 - core),
            weight(far_side + core),
            weight(far_side + 1 - core),
        ]

    def parity(k, _):
        if "weights" not in shares:
            shares["weights"] = weights()
        by_slot = shares["weights"]
        for piece in pieces(k):
            shares[piece][1].wait()
            mine = pl.ds(piece[0], PIECE)
            total = by_slot[0] * shared.at[0, mine][...]
            for slot in range(1, 3):
                total = total + by_slot[slot] * shared.at[slot, mine][...]
            shares[piece][2].wait()
            results.at[3, mine][...] = total + by_slot[3] * shared.at[3, mine][...]

    steps = {
        "l": load,
        "g": lambda k, u: give_peer(k, UNITS[u], (FAR,), given(k, 0, u)),
        "h": lambda k, u: give_peer(k, UNITS[u], (AFTER, BEFORE), given(k, 1, u)),
        "G": lambda k, g: give_peer(k, LOADS[g], (OWN,), given(k, 2, g)),
        "b": lambda k, u: send_far(k, 0, u),
        "c": lambda k, u: send_near(k, 0, u),
        "d": lambda k, u: pass_on(k, 0, u),
        "o": lambda k, u: finish(k, 0, u),
        "F": lambda k, u: send_far(k, 1, u),
        "N": lambda k, u: send_near(k, 1, u),
        "D": lambda k, u: pass_on(k, 1, u),
        "O": lambda k, u: finish(k, 1, u),
        "f": lambda k, u: send_far(k, 2, u),
        "n": lambda k, u: send_near(k, 2, u),
        "e": lambda k, u: pass_on(k, 2, u),
        "q": step_params,
        "r": relay,
        "t": parity,
    }

    barrier = pltpu.get_barrier_semaphore()
    for to in ahead + behind + [other_core]:
        pl.semaphore_signal(barrier, inc=1, device_id=to, device_id_type=MESH)
    for g in range(4):
        load(0, g)
    for i, ref in enumerate((params, one, two)):
        pltpu.make_async_copy(ref, state.at[i], misc.at[i]).start()
    pltpu.make_async_copy(coding, codes, misc.at[3]).start()
    pltpu.make_async_copy(holders, held, misc.at[4]).start()
    pl.semaphore_wait(barrier, 7)
    plan = " ".join(PLAN).split()
    for step in plan:
        if step[1] == "t" and step == [s for s in plan if s[1] == "t"][-1]:
            for k in range(len(CHUNKS)):
                arrived(bufs[k][0], peer_send.at[k])
                arrived(bufs[k][0].at[pl.ds(0, 3)], link_send.at[3 * k])
                arrived(bufs[k][0].at[pl.ds(0, 3), 0], link_send.at[3 * k + 1])
                arrived(bufs[k][0].at[pl.ds(0, 3), 0, 0], link_send.at[3 * k + 2])
        steps[step[1]](int(step[0]), int(step[2]) - 1)


def write(results, *rest):
    outs, sems = rest[:-1], rest[-1]
    copies = [pltpu.make_async_copy(results.at[i], out, sems.at[i]) for i, out in enumerate(outs)]
    for copy in copies:
        copy.start()
    for copy in copies:
        copy.wait()


def shards(grads, params, moment_one, moment_two, coding, holders):
    rows = grads.shape[2] // LANES
    partial = grads.reshape(4, rows, LANES).transpose(1, 0, 2)
    flat = lambda t: t.reshape(ROWS, LANES)
    anywhere = pl.BlockSpec(memory_space=pltpu.HBM)
    vmem = pl.BlockSpec(memory_space=pltpu.VMEM)
    f32 = jnp.float32
    scratch = []
    for _, sizes in CHUNKS:
        n = sum(sizes)
        for lead in ((4, 4, 4), (4, 4, 4), (4, 4), (2, 4, 4), (4,), (2, 4), (), (2,)):
            scratch.append(pltpu.VMEM(lead + (n, LANES), f32))
    chunks = len(CHUNKS)
    scratch += [
        pltpu.VMEM((3, ROWS, LANES), f32),
        pltpu.VMEM((4, ROWS, LANES), f32),
        pltpu.SMEM((2, 4), f32),
        pltpu.SMEM((1, 2), jnp.int32),
        pltpu.SemaphoreType.DMA((chunks * 3,)),
        pltpu.SemaphoreType.DMA((chunks * PER_CHUNK * 2,)),
        pltpu.SemaphoreType.DMA((chunks * len(LOADS),)),
        pltpu.SemaphoreType.DMA((chunks * GIVEN,)),
        pltpu.SemaphoreType.DMA((chunks,)),
        pltpu.SemaphoreType.DMA((5 + 6 * (ROWS // PIECE),)),
    ]
    results = pl.pallas_call(
        kernel,
        out_shape=pltpu.VMEM((4, ROWS, LANES), f32),
        in_specs=[anywhere] * 6,
        out_specs=vmem,
        scratch_shapes=scratch,
        compiler_params=pltpu.CompilerParams(
            collective_id=0, has_side_effects=True, vmem_limit_bytes=56 * 1024 * 1024
        ),
    )(partial, flat(params), flat(moment_one), flat(moment_two), coding.T, holders)
    out = pl.pallas_call(
        write,
        out_shape=[jax.ShapeDtypeStruct((ROWS, LANES), f32)] * 4,
        in_specs=[vmem],
        out_specs=[anywhere] * 4,
        scratch_shapes=[pltpu.SemaphoreType.DMA((4,))],
    )(pltpu.with_memory_space_constraint(results, pltpu.VMEM))
    return tuple(t.reshape(1, ROWS * LANES) for t in out)


def solution(mesh):
    return jax.shard_map(
        shards,
        mesh=mesh,
        in_specs=(
            P(("group", "fsdp"), None, None),
            P("group", "fsdp"),
            P("group", "fsdp"),
            P("group", "fsdp"),
            P(),
            P("fsdp", None),
        ),
        out_specs=(P("group", "fsdp"), P("group", "fsdp"), P("group", "fsdp"), P("group", "fsdp")),
        check_vma=False,
    )
```

```python
import jax
import jax.numpy as jnp
from jax import lax
from jax.experimental import pallas as pl
from jax.experimental.pallas import tpu as pltpu
from jax.sharding import PartitionSpec as P

MESH = pl.DeviceIdType.MESH
LANES = 128
ROWS = 256
STEP = (2, 3, 1, 0)
FAR, BEFORE, AFTER, OWN = range(4)
ORDERS = ((0, 1, 2), (1, 2, 0), (2, 0, 1))
HALF = ROWS // 2
CHUNKS = ((0, (64, 64, 64)), (96, (24, 16, 24)))
FINE = (
    ((0, 1), (0, 1)),
    ((0, 1), (1, 2)),
    ((1, 2), (0, 1)),
    ((1, 2), (1, 2)),
    ((0, 1), (3, 1)),
    ((3, 1), (0, 1)),
    ((3, 1), (1, 2)),
    ((1, 2), (3, 1)),
    ((3, 1), (3, 1)),
)
COARSE = (((0, 3), (0, 3)), ((0, 3), (3, 1)), ((3, 1), (0, 3)), ((3, 1), (3, 1)))
UNITS = (FINE, COARSE,)
RANGES = tuple((((0, 1),), ((1, 2),), ((3, 1),)) if units is FINE else (((0, 3),), ((3, 1),)) for units in UNITS)
STAGES = tuple((units, ranges, ((),)) for units, ranges in zip(UNITS, RANGES))
LOADS = (
    (((0, 1), (0, 1)), ((0, 1), (1, 3)), ((1, 2), (0, 4)), ((3, 1), (0, 4))),
    (((0, 4), (0, 4)),),
)


def load_of(k, u):
    inside = lambda small, big: all(b[0] <= s[0] and s[0] + s[1] <= b[0] + b[1] for s, b in zip(small, big))
    return [inside(UNITS[k][u], group) for group in LOADS[k]].index(True)


LANDINGS = [2 * sum(len(units) for units in stages) for stages in STAGES]
GIVEN = [2 * len(units) + len(loads) for units, loads in zip(UNITS, LOADS)]
LOADED = [len(loads) for loads in LOADS]
PLAN = (
    "0g2 0g4 0g1 0h2",
    "1g1 0h4 0b2 0G2",
    "0b4 1l1 0g6 0h1",
    "0G3 0b1 0c2 1b1",
    "0g3 1h1 0c4 0G1",
    "0d2 1g3 0h6 1G1",
    "0g5 0b6 0d4 0h3",
    "0G4 1g2 1h3 0g8",
    "0c1 0d1 0h5 0g7",
    "0b3 1h2 1g4 0h8",
    "1c1 1d1 0g9 0h7",
    "1h4 0h9 0o2 0F2",
    "1b3 0o4 0N2 0o1",
    "0F1 0c6 0d6 0b5",
    "0c3 0d3 1o1 1F1",
    "1N1 0D2 1b2 1c3",
    "1d3 0b8 0o6 0c5",
    "0d5 0b7 0o3 0N1",
    "0D1 1D1 1c2 1b4",
    "0c8 1d2 1o3 0b9",
    "0c7 0d8 0o5 0F3",
    "0d7 0O1 0f1 1O1",
    "1f1 1n1 1c4 1d4",
    "0c9 1o2 1F2 1N2",
    "0d9 0o8 0N3 0D3",
    "0o7 0O2 0n1 0e1",
    "1e1 1D2 0q1 1q1",
    "1t1 0t1",
)


def device(x, y, z, core):
    return {"group": y % 2 * 2 + core, "fsdp": y // 2 * 16 + x * 4 + z}


def kernel(grads, params, one, two, coding, holders, results, *scratch):
    bufs = [scratch[12 * k : 12 * k + 12] for k in range(len(CHUNKS))]
    state, codes, held, link_send, link_recv, own_sem, peer_sem, peer_send, misc = scratch[12 * len(CHUNKS) :]
    group, fsdp = lax.axis_index("group"), lax.axis_index("fsdp")
    core = group % 2
    here = (fsdp // 4 % 4, fsdp // 16 * 2 + group // 2, fsdp % 4)

    def along(axis, distance):
        there = list(here)
        there[axis] = (there[axis] + distance) % 4
        return device(*there, core)

    ahead = [along(axis, 1) for axis in range(3)]
    behind = [along(axis, 3) for axis in range(3)]
    other_core = device(*here, 1 - core)
    across = [device(here[0], here[1] // 2 * 2 + 1 - here[1] % 2, here[2], c) for c in range(2)]
    across_other = device(here[0], here[1] // 2 * 2 + 1 - here[1] % 2, here[2], 1 - core)

    places = [[(here[axis] + d) % 4 for d in STEP] for axis in range(3)]
    starts = (
        [v * (4 * ROWS) for v in places[0]],
        [v // 2 * (16 * ROWS) for v in places[1]],
        [v * ROWS for v in places[2]],
    )
    group_rows = [v % 2 * 2 for v in places[1]]

    def parts_of(k, odd=0):
        first, sizes = CHUNKS[k]
        out, at_row = [], 0
        for order, rows in zip(ORDERS, sizes):
            cut = 8 * ((rows // 8 + odd) // 2)
            out.append((order, at_row, at_row + cut, at_row + rows, first + at_row))
            at_row += rows
        return out

    def slots_of(unit):
        out = [()]
        for first, count in unit:
            out = [s + (i,) for s in out for i in range(first, first + count)]
        return out

    def at(ref, lead, unit, rows=None):
        index = tuple(lead) + tuple(pl.ds(first, count) for first, count in unit)
        if rows is not None:
            index += (pl.ds(rows[0], rows[1] - rows[0]),)
        return ref.at[index] if index else ref

    def arrived(ref, sem):
        pltpu.make_async_copy(ref, ref, sem).wait()

    def terms(k, slots, which):
        each = sum(CHUNKS[k][1]) // 2
        for order, low, _, high, first in parts_of(k):
            slot = {axis: slots[i] for i, axis in enumerate(order)}
            start = starts[0][slot[0]] + starts[1][slot[1]] + starts[2][slot[2]] + which * HALF + CHUNKS[k][0]
            for g in range(2):
                begin, end = max(low, g * each), min(high, (g + 1) * each)
                if begin < end:
                    rows = pl.ds(pl.multiple_of(start + (begin - g * each), 8), end - begin)
                    yield grads.at[rows, group_rows[slot[1]] + g], slots + (pl.ds(begin, end - begin),)

    def load(k, g):
        for m in range(4):
            for s in slots_of(LOADS[k][g]):
                for source, place in terms(k, (m,) + s, core):
                    pltpu.make_async_copy(source, bufs[k][0].at[place], own_sem.at[sum(LOADED[:k]) + g]).start()

    def give_peer(k, block, slots, sem):
        for m in slots:
            for s in slots_of(block):
                for source, place in terms(k, (m,) + s, 1 - core):
                    pltpu.make_async_remote_copy(
                        src_ref=source,
                        dst_ref=bufs[k][1].at[place],
                        send_sem=peer_send.at[k],
                        recv_sem=sem,
                        device_id=other_core,
                        device_id_type=MESH,
                    ).start()

    def given(k, kind, i):
        return peer_sem.at[sum(GIVEN[:k]) + kind * len(UNITS[k]) + i]

    waited = set()

    def ready(k, u, kind):
        g = load_of(k, u)
        if (k, g) not in waited:
            waited.add((k, g))
            arrived(at(bufs[k][0], (), ((0, 4),) + LOADS[k][g]), own_sem.at[sum(LOADED[:k]) + g])
        if kind < 2:
            slots = ((0, 1), (1, 2))[kind]
            arrived(at(bufs[k][1], (), (slots,) + UNITS[k][u]), given(k, kind, u))
        elif (k, g, OWN) not in waited:
            waited.add((k, g, OWN))
            arrived(at(bufs[k][1], (OWN,), LOADS[k][g]), given(k, 2, g))

    def add(refs):
        total = refs[0][...]
        for ref in refs[1:]:
            total = total + ref[...]
        refs[0][...] = total

    def landing(k, stage, u, kind):
        return link_recv.at[sum(LANDINGS[:k]) + 2 * (sum(len(units) for units in STAGES[k][:stage]) + u) + kind]

    def send(k, stage, u, kind, source, target, to):
        pltpu.make_async_remote_copy(
            src_ref=source,
            dst_ref=target,
            send_sem=link_send.at[3 * k + stage],
            recv_sem=landing(k, stage, u, kind),
            device_id=to,
            device_id_type=MESH,
        ).start()

    def values(k, stage, u, slot, rows):
        return at(bufs[k][0], (OWN,) * stage + (slot,), STAGES[k][stage][u], rows)

    def far(k, stage, u, rows=None):
        return at(bufs[k][2 + 2 * stage], (), STAGES[k][stage][u], rows)

    def near(k, stage, u, way, rows=None):
        return at(bufs[k][3 + 2 * stage], (way,), STAGES[k][stage][u], rows)

    def sum_up(k, stage, u, slot, rows, others):
        lead = (OWN,) * stage + (slot,)
        here_rows = (pl.ds(rows[0], rows[1] - rows[0]),)
        for s in slots_of(STAGES[k][stage][u]):
            refs = [bufs[k][0].at[lead + s + here_rows]]
            if stage == 0:
                refs.append(bufs[k][1].at[lead + s + here_rows])
            refs += [ref.at[extra + s + here_rows] for ref, extra in others]
            if len(refs) > 1:
                add(refs)

    def send_far(k, stage, u):
        whole = (0, sum(CHUNKS[k][1]))
        if stage == 0:
            ready(k, u, 0)
        sum_up(k, stage, u, FAR, whole, [])
        for order, low, cut, high, _ in parts_of(k, u % 2):
            axis = order[stage]
            for rows, to in (((low, cut), ahead[axis]), ((cut, high), behind[axis])):
                send(k, stage, u, 0, values(k, stage, u, FAR, rows), far(k, stage, u, rows), to)

    def send_near(k, stage, u):
        if stage == 0:
            ready(k, u, 1)
        for order, low, cut, high, _ in parts_of(k, u % 2):
            axis = order[stage]
            for slot, way, rows, to in ((AFTER, 0, (cut, high), ahead[axis]), (BEFORE, 1, (low, cut), behind[axis])):
                sum_up(k, stage, u, slot, rows, [])
                send(k, stage, u, 1, values(k, stage, u, slot, rows), near(k, stage, u, way, rows), to)

    def pass_on(k, stage, u):
        arrived(far(k, stage, u), landing(k, stage, u, 0))
        for order, low, cut, high, _ in parts_of(k, u % 2):
            axis = order[stage]
            for slot, way, rows, to in ((AFTER, 0, (low, cut), ahead[axis]), (BEFORE, 1, (cut, high), behind[axis])):
                sum_up(k, stage, u, slot, rows, [(bufs[k][2 + 2 * stage], ())])
                send(k, stage, u, 1, values(k, stage, u, slot, rows), near(k, stage, u, way, rows), to)

    def finish(k, stage, u):
        if stage == 0:
            ready(k, u, 2)
        arrived(at(bufs[k][3 + 2 * stage], (), ((0, 2),) + STAGES[k][stage][u]), landing(k, stage, u, 1))
        landed = bufs[k][3 + 2 * stage]
        sum_up(k, stage, u, OWN, (0, sum(CHUNKS[k][1])), [(landed, (0,)), (landed, (1,))])

    def weights():
        arrived(codes, misc.at[2])
        arrived(held, misc.at[3])
        none = jnp.float32(0.0)
        first = group // 2 * 2
        opposite = 2 - first
        return [
            [
                jnp.where(held[0, 0] == d, codes[0, first + g], none)
                + jnp.where(held[0, 1] == d, codes[1, first + g], none)
                for g in range(2)
            ]
            for d in (group, first + 1 - core, opposite, opposite + 1)
        ]

    known = {}

    def push(k, source, target, kind, to):
        pltpu.make_async_remote_copy(
            src_ref=source,
            dst_ref=target,
            send_sem=misc.at[4 + 3 * k],
            recv_sem=misc.at[5 + 3 * k + kind],
            device_id=to,
            device_id_type=MESH,
        ).start()

    def step_params(k, _):
        if not known:
            for g, sem in ((core, misc.at[0]), (1 - core, misc.at[1])):
                arrived(state.at[g], sem)
            known["weights"] = weights()
        finish(k, 0, len(UNITS[k]) - 1)
        finish(k, 1, len(RANGES[k]) - 1)
        finish(k, 2, 0)
        new, sums, beside, landed = bufs[k][8:]
        each = sum(CHUNKS[k][1]) // 2
        mine = pl.ds(CHUNKS[k][0], each)
        first_fix = 1.0 - 0.9**10
        second_fix = 1.0 - 0.95**10
        new_params = []
        for g in range(2):
            gradient = bufs[k][0].at[OWN, OWN, OWN, pl.ds(g * each, each)][...]
            values = state.at[g, 0, mine][...]
            first_moment = 0.9 * state.at[g, 1, mine][...] + 0.1 * gradient
            second_moment = 0.95 * state.at[g, 2, mine][...] + 0.05 * gradient * gradient
            update = first_moment / first_fix / (jnp.sqrt(second_moment / second_fix) + 1e-08) + 0.1 * values
            new_params.append(values - 0.05 * update)
            new.at[g, 0][...] = new_params[g]
            new.at[g, 1][...] = first_moment
            new.at[g, 2][...] = second_moment
        total = lambda w: w[0] * new_params[0] + w[1] * new_params[1]
        by_device = known["weights"]
        for c in range(2):
            sums.at[2 + c][...] = total(by_device[2 + c])
            push(k, sums.at[2 + c], landed.at[core], 1, across[c])
        sums.at[1][...] = total(by_device[1])
        push(k, sums.at[1], beside.at[3], 0, other_core)
        push(k, new.at[1 - core], beside.at[pl.ds(0, 3)], 0, other_core)
        sums.at[0][...] = total(by_device[0])
        place = rows_in(k, core)
        for i in range(3):
            results.at[i, place][...] = new.at[core, i][...]

    def rows_in(k, which):
        return pl.ds(pl.multiple_of(which * HALF + CHUNKS[k][0], 8), sum(CHUNKS[k][1]) // 2)

    def parity(k, _):
        new, sums, beside, landed = bufs[k][8:]
        arrived(beside, misc.at[5 + 3 * k])
        place, other = rows_in(k, core), rows_in(k, 1 - core)
        for i in range(3):
            results.at[i, other][...] = beside.at[i][...]
        arrived(landed, misc.at[6 + 3 * k])
        results.at[3, place][...] = sums.at[0][...] + landed.at[core][...]
        results.at[3, other][...] = beside.at[3][...] + landed.at[1 - core][...]

    steps = {
        "l": load,
        "g": lambda k, u: give_peer(k, UNITS[k][u], (FAR,), given(k, 0, u)),
        "h": lambda k, u: give_peer(k, UNITS[k][u], (AFTER, BEFORE), given(k, 1, u)),
        "G": lambda k, g: give_peer(k, LOADS[k][g], (OWN,), given(k, 2, g)),
        "b": lambda k, u: send_far(k, 0, u),
        "c": lambda k, u: send_near(k, 0, u),
        "d": lambda k, u: pass_on(k, 0, u),
        "o": lambda k, u: finish(k, 0, u),
        "F": lambda k, u: send_far(k, 1, u),
        "N": lambda k, u: send_near(k, 1, u),
        "D": lambda k, u: pass_on(k, 1, u),
        "O": lambda k, u: finish(k, 1, u),
        "f": lambda k, u: send_far(k, 2, u),
        "n": lambda k, u: send_near(k, 2, u),
        "e": lambda k, u: pass_on(k, 2, u),
        "q": step_params,
        "t": parity,
    }

    barrier = pltpu.get_barrier_semaphore()
    for to in ahead + behind + [other_core, across_other]:
        pl.semaphore_signal(barrier, inc=1, device_id=to, device_id_type=MESH)
    for g in range(len(LOADS[0])):
        load(0, g)
    own_half, other_half = (pl.ds(pl.multiple_of(c * HALF, 8), HALF) for c in (core, 1 - core))
    for i, ref in enumerate((params, one, two)):
        pltpu.make_async_copy(ref.at[own_half], state.at[core, i], misc.at[0]).start()
    pltpu.make_async_copy(coding, codes, misc.at[2]).start()
    pltpu.make_async_copy(holders, held, misc.at[3]).start()
    pl.semaphore_wait(barrier, 8)
    plan = " ".join(PLAN).split()
    early = 12
    for number, step in enumerate(plan):
        if number == early:
            for i, ref in enumerate((params, one, two)):
                pltpu.make_async_remote_copy(
                    src_ref=ref.at[other_half],
                    dst_ref=state.at[core, i],
                    send_sem=misc.at[4 + 3 * len(CHUNKS)],
                    recv_sem=misc.at[1],
                    device_id=other_core,
                    device_id_type=MESH,
                ).start()
        if step[1] == "t" and step == [s for s in plan if s[1] == "t"][-1]:
            arrived(state.at[0], misc.at[4 + 3 * len(CHUNKS)])
            for k in range(len(CHUNKS)):
                arrived(bufs[k][0], peer_send.at[k])
                arrived(bufs[k][0].at[pl.ds(0, 3)], link_send.at[3 * k])
                arrived(bufs[k][0].at[pl.ds(0, 3), 0], link_send.at[3 * k + 1])
                arrived(bufs[k][0].at[pl.ds(0, 3), 0, 0], link_send.at[3 * k + 2])
        steps[step[1]](int(step[0]), int(step[2]) - 1)
    for k in range(len(CHUNKS)):
        arrived(bufs[k][8], misc.at[4 + 3 * k])


def write(results, *rest):
    outs, sems = rest[:-1], rest[-1]
    copies = [pltpu.make_async_copy(results.at[i], out, sems.at[i]) for i, out in enumerate(outs)]
    for copy in copies:
        copy.start()
    for copy in copies:
        copy.wait()


def shards(grads, params, moment_one, moment_two, coding, holders):
    rows = grads.shape[2] // LANES
    partial = grads.reshape(4, rows, LANES).transpose(1, 0, 2)
    flat = lambda t: t.reshape(ROWS, LANES)
    anywhere = pl.BlockSpec(memory_space=pltpu.HBM)
    vmem = pl.BlockSpec(memory_space=pltpu.VMEM)
    f32 = jnp.float32
    scratch = []
    for _, sizes in CHUNKS:
        n = sum(sizes)
        for lead in ((4, 4, 4), (4, 4, 4), (4, 4), (2, 4, 4), (4,), (2, 4), (), (2,)):
            scratch.append(pltpu.VMEM(lead + (n, LANES), f32))
        for lead in ((2, 3), (4,), (4,), (2,)):
            scratch.append(pltpu.VMEM(lead + (n // 2, LANES), f32))
    chunks = len(CHUNKS)
    scratch += [
        pltpu.VMEM((2, 3, HALF, LANES), f32),
        pltpu.SMEM((2, 4), f32),
        pltpu.SMEM((1, 2), jnp.int32),
        pltpu.SemaphoreType.DMA((chunks * 3,)),
        pltpu.SemaphoreType.DMA((sum(LANDINGS),)),
        pltpu.SemaphoreType.DMA((sum(LOADED),)),
        pltpu.SemaphoreType.DMA((sum(GIVEN),)),
        pltpu.SemaphoreType.DMA((chunks,)),
        pltpu.SemaphoreType.DMA((5 + 3 * chunks,)),
    ]
    results = pl.pallas_call(
        kernel,
        out_shape=pltpu.VMEM((4, ROWS, LANES), f32),
        in_specs=[anywhere] * 6,
        out_specs=vmem,
        scratch_shapes=scratch,
        compiler_params=pltpu.CompilerParams(
            collective_id=0, has_side_effects=True, vmem_limit_bytes=56 * 1024 * 1024
        ),
    )(partial, flat(params), flat(moment_one), flat(moment_two), coding.T, holders)
    out = pl.pallas_call(
        write,
        out_shape=[jax.ShapeDtypeStruct((ROWS, LANES), f32)] * 4,
        in_specs=[vmem],
        out_specs=[anywhere] * 4,
        scratch_shapes=[pltpu.SemaphoreType.DMA((4,))],
    )(pltpu.with_memory_space_constraint(results, pltpu.VMEM))
    return tuple(t.reshape(1, ROWS * LANES) for t in out)


def solution(mesh):
    return jax.shard_map(
        shards,
        mesh=mesh,
        in_specs=(
            P(("group", "fsdp"), None, None),
            P("group", "fsdp"),
            P("group", "fsdp"),
            P("group", "fsdp"),
            P(),
            P("fsdp", None),
        ),
        out_specs=(P("group", "fsdp"), P("group", "fsdp"), P("group", "fsdp"), P("group", "fsdp")),
        check_vma=False,
    )
```

```python
import jax
import jax.numpy as jnp
from jax import lax
from jax.experimental import pallas as pl
from jax.experimental.pallas import tpu as pltpu
from jax.sharding import PartitionSpec as P

MESH = pl.DeviceIdType.MESH
LANES = 128
ROWS = 256
STEP = (2, 3, 1, 0)
FAR, BEFORE, AFTER, OWN = range(4)
ORDERS = ((0, 1, 2), (1, 2, 0), (2, 0, 1), (2, 1, 0))
HALF = ROWS // 2
CHUNKS = ((0, (64, 64, 48, 16)), (96, (24, 16, 16, 8)))
FINE = (
    ((0, 1), (0, 1)),
    ((0, 1), (1, 2)),
    ((1, 2), (0, 1)),
    ((1, 2), (1, 2)),
    ((0, 1), (3, 1)),
    ((3, 1), (0, 1)),
    ((3, 1), (1, 2)),
    ((1, 2), (3, 1)),
    ((3, 1), (3, 1)),
)
COARSE = (((0, 3), (0, 3)), ((0, 3), (3, 1)), ((3, 1), (0, 3)), ((3, 1), (3, 1)))
UNITS = (FINE, COARSE,)
RANGES = tuple((((0, 1),), ((1, 2),), ((3, 1),)) if units is FINE else (((0, 3),), ((3, 1),)) for units in UNITS)
STAGES = tuple((units, ranges, ((),)) for units, ranges in zip(UNITS, RANGES))
LOADS = (
    (((0, 1), (0, 1)), ((0, 1), (1, 3)), ((1, 2), (0, 4)), ((3, 1), (0, 4))),
    (((0, 4), (0, 4)),),
)


def load_of(k, u):
    inside = lambda small, big: all(b[0] <= s[0] and s[0] + s[1] <= b[0] + b[1] for s, b in zip(small, big))
    return [inside(UNITS[k][u], group) for group in LOADS[k]].index(True)


LANDINGS = [2 * sum(len(units) for units in stages) for stages in STAGES]
GIVEN = [2 * len(units) + len(loads) for units, loads in zip(UNITS, LOADS)]
LOADED = [len(loads) for loads in LOADS]
RAW = (0, 1)
PLAN = (
    "0b2 0g4 0g1 0h2",
    "1g1 0h4 0G2 0b4",
    "1l1 0g6 0h1 0G3",
    "0b1 0c2 1b1 0g3",
    "1h1 0c4 0G1 0x2",
    "1g3 0h6 1G1 0g5",
    "0b6 0d4 0d2 0h3",
    "0G4 1g2 1h3 0g8",
    "0c1 0d1 0h5 0g7",
    "0b3 1h2 1g4 0h8",
    "1c1 1d1 0g9 0h7",
    "1h4 0h9 0o2 0F2",
    "1b3 0o4 0N2 0o1",
    "0F1 0c6 0d6 0b5",
    "0c3 0d3 1o1 1F1",
    "1N1 0D2 1b2 1c3",
    "1d3 0b8 0o6 0c5",
    "0d5 0b7 0o3 0N1",
    "0D1 1D1 1c2 1b4",
    "0c8 1d2 1o3 0b9",
    "0c7 0d8 0o5 0F3",
    "0d7 0O1 0f1 1O1",
    "1f1 1n1 1c4 1d4",
    "0c9 1o2 1F2 1N2",
    "0d9 0o8 0N3 0D3",
    "0o7 0O2 0n1 0e1",
    "1e1 1D2 0q1 1q1",
    "1t1 0t1",
)


def device(x, y, z, core):
    return {"group": y % 2 * 2 + core, "fsdp": y // 2 * 16 + x * 4 + z}


def kernel(grads, params, one, two, coding, holders, results, *scratch):
    bufs = [scratch[12 * k : 12 * k + 12] for k in range(len(CHUNKS))]
    state, early, late, codes, held, link_send, link_recv, own_sem, peer_sem, peer_send, misc = scratch[12 * len(CHUNKS) :]
    group, fsdp = lax.axis_index("group"), lax.axis_index("fsdp")
    core = group % 2
    here = (fsdp // 4 % 4, fsdp // 16 * 2 + group // 2, fsdp % 4)

    def along(axis, distance):
        there = list(here)
        there[axis] = (there[axis] + distance) % 4
        return device(*there, core)

    ahead = [along(axis, 1) for axis in range(3)]
    behind = [along(axis, 3) for axis in range(3)]
    other_core = device(*here, 1 - core)
    across = [device(here[0], here[1] // 2 * 2 + 1 - here[1] % 2, here[2], c) for c in range(2)]
    across_other = device(here[0], here[1] // 2 * 2 + 1 - here[1] % 2, here[2], 1 - core)

    places = [[(here[axis] + d) % 4 for d in STEP] for axis in range(3)]
    starts = (
        [v * (4 * ROWS) for v in places[0]],
        [v // 2 * (16 * ROWS) for v in places[1]],
        [v * ROWS for v in places[2]],
    )
    group_rows = [v % 2 * 2 for v in places[1]]

    def parts_of(k, odd=0):
        first, sizes = CHUNKS[k]
        out, at_row = [], 0
        for order, rows in zip(ORDERS, sizes):
            if rows == 0:
                continue
            cut = 8 * ((rows // 8 + odd) // 2)
            out.append((order, at_row, at_row + cut, at_row + rows, first + at_row))
            at_row += rows
        return out

    def slots_of(unit):
        out = [()]
        for first, count in unit:
            out = [s + (i,) for s in out for i in range(first, first + count)]
        return out

    def at(ref, lead, unit, rows=None):
        index = tuple(lead) + tuple(pl.ds(first, count) for first, count in unit)
        if rows is not None:
            index += (pl.ds(rows[0], rows[1] - rows[0]),)
        return ref.at[index] if index else ref

    def arrived(ref, sem):
        pltpu.make_async_copy(ref, ref, sem).wait()

    def terms(k, slots, which, odd=0, way=None):
        each = sum(CHUNKS[k][1]) // 2
        for order, low, cut, high, first in parts_of(k, odd):
            if way is not None:
                low, high = ((low, cut), (cut, high))[way]
            slot = {axis: slots[i] for i, axis in enumerate(order)}
            start = starts[0][slot[0]] + starts[1][slot[1]] + starts[2][slot[2]] + which * HALF + CHUNKS[k][0]
            for g in range(2):
                begin, end = max(low, g * each), min(high, (g + 1) * each)
                if begin < end:
                    rows = pl.ds(pl.multiple_of(start + (begin - g * each), 8), end - begin)
                    yield grads.at[rows, group_rows[slot[1]] + g], slots + (pl.ds(begin, end - begin),), order[0]

    def load(k, g):
        for m in range(4):
            for s in slots_of(LOADS[k][g]):
                for source, place, _ in terms(k, (m,) + s, core):
                    pltpu.make_async_copy(source, bufs[k][0].at[place], own_sem.at[sum(LOADED[:k]) + g]).start()

    def give_peer(k, block, slots, sem):
        for m in slots:
            for s in slots_of(block):
                for source, place, _ in terms(k, (m,) + s, 1 - core):
                    pltpu.make_async_remote_copy(
                        src_ref=source,
                        dst_ref=bufs[k][1].at[place],
                        send_sem=peer_send.at[k],
                        recv_sem=sem,
                        device_id=other_core,
                        device_id_type=MESH,
                    ).start()

    def given(k, kind, i):
        return peer_sem.at[sum(GIVEN[:k]) + kind * len(UNITS[k]) + i]

    waited = set()

    def ready(k, u, kind):
        g = load_of(k, u)
        if (k, g) not in waited:
            waited.add((k, g))
            arrived(at(bufs[k][0], (), ((0, 4),) + LOADS[k][g]), own_sem.at[sum(LOADED[:k]) + g])
        if kind < 2:
            slots = ((0, 1), (1, 2))[kind]
            arrived(at(bufs[k][1], (), (slots,) + UNITS[k][u]), given(k, kind, u))
        elif (k, g, OWN) not in waited:
            waited.add((k, g, OWN))
            arrived(at(bufs[k][1], (OWN,), LOADS[k][g]), given(k, 2, g))

    def add(refs):
        total = refs[0][...]
        for ref in refs[1:]:
            total = total + ref[...]
        refs[0][...] = total

    def landing(k, stage, u, kind):
        return link_recv.at[sum(LANDINGS[:k]) + 2 * (sum(len(units) for units in STAGES[k][:stage]) + u) + kind]

    def send(k, stage, u, kind, source, target, to):
        pltpu.make_async_remote_copy(
            src_ref=source,
            dst_ref=target,
            send_sem=link_send.at[3 * k + stage],
            recv_sem=landing(k, stage, u, kind),
            device_id=to,
            device_id_type=MESH,
        ).start()

    def values(k, stage, u, slot, rows):
        return at(bufs[k][0], (OWN,) * stage + (slot,), STAGES[k][stage][u], rows)

    def far(k, stage, u, rows=None):
        return at(bufs[k][2 + 2 * stage], (), STAGES[k][stage][u], rows)

    def near(k, stage, u, way, rows=None):
        return at(bufs[k][3 + 2 * stage], (way,), STAGES[k][stage][u], rows)

    def sum_up(k, stage, u, slot, rows, others):
        lead = (OWN,) * stage + (slot,)
        here_rows = (pl.ds(rows[0], rows[1] - rows[0]),)
        for s in slots_of(STAGES[k][stage][u]):
            refs = [bufs[k][0].at[lead + s + here_rows]]
            if stage == 0:
                refs.append(bufs[k][1].at[lead + s + here_rows])
            refs += [ref.at[extra + s + here_rows] for ref, extra in others]
            if len(refs) > 1:
                add(refs)

    def send_far(k, stage, u):
        whole = (0, sum(CHUNKS[k][1]))
        if stage == 0:
            ready(k, u, 0)
        sum_up(k, stage, u, FAR, whole, [])
        for order, low, cut, high, _ in parts_of(k, u % 2):
            axis = order[stage]
            for rows, to in (((low, cut), ahead[axis]), ((cut, high), behind[axis])):
                if rows[0] == rows[1]:
                    continue
                send(k, stage, u, 0, values(k, stage, u, FAR, rows), far(k, stage, u, rows), to)

    def send_raw(k, u):
        for which, target, kinds in (
            (core, bufs[k][2], (link_send.at[3 * k], landing(k, 0, u, 0))),
            (1 - core, early, (misc.at[5 + 3 * len(CHUNKS)], misc.at[6 + 3 * len(CHUNKS)])),
        ):
            for s in slots_of(UNITS[k][u]):
                for way, to in enumerate((ahead, behind)):
                    for source, place, axis in terms(k, (FAR,) + s, which, u % 2, way):
                        pltpu.make_async_remote_copy(
                            src_ref=source,
                            dst_ref=target.at[place[1:]],
                            send_sem=kinds[0],
                            recv_sem=kinds[1],
                            device_id=to[axis],
                            device_id_type=MESH,
                        ).start()

    def hand_over(k, u):
        arrived(at(early, (), UNITS[k][u]), misc.at[6 + 3 * len(CHUNKS)])
        pltpu.make_async_remote_copy(
            src_ref=at(early, (), UNITS[k][u]),
            dst_ref=at(late, (), UNITS[k][u]),
            send_sem=peer_send.at[k],
            recv_sem=misc.at[7 + 3 * len(CHUNKS)],
            device_id=other_core,
            device_id_type=MESH,
        ).start()

    def send_near(k, stage, u):
        if stage == 0:
            ready(k, u, 1)
        for order, low, cut, high, _ in parts_of(k, u % 2):
            axis = order[stage]
            for slot, way, rows, to in ((AFTER, 0, (cut, high), ahead[axis]), (BEFORE, 1, (low, cut), behind[axis])):
                if rows[0] == rows[1]:
                    continue
                sum_up(k, stage, u, slot, rows, [])
                send(k, stage, u, 1, values(k, stage, u, slot, rows), near(k, stage, u, way, rows), to)

    def pass_on(k, stage, u):
        arrived(far(k, stage, u), landing(k, stage, u, 0))
        came = [(bufs[k][2 + 2 * stage], ())]
        if stage == 0 and (k, u) == RAW:
            arrived(at(late, (), UNITS[k][u]), misc.at[7 + 3 * len(CHUNKS)])
            came.append((late, ()))
        for order, low, cut, high, _ in parts_of(k, u % 2):
            axis = order[stage]
            for slot, way, rows, to in ((AFTER, 0, (low, cut), ahead[axis]), (BEFORE, 1, (cut, high), behind[axis])):
                if rows[0] == rows[1]:
                    continue
                sum_up(k, stage, u, slot, rows, came)
                send(k, stage, u, 1, values(k, stage, u, slot, rows), near(k, stage, u, way, rows), to)

    def finish(k, stage, u):
        if stage == 0:
            ready(k, u, 2)
        arrived(at(bufs[k][3 + 2 * stage], (), ((0, 2),) + STAGES[k][stage][u]), landing(k, stage, u, 1))
        landed = bufs[k][3 + 2 * stage]
        sum_up(k, stage, u, OWN, (0, sum(CHUNKS[k][1])), [(landed, (0,)), (landed, (1,))])

    def weights():
        arrived(codes, misc.at[2])
        arrived(held, misc.at[3])
        none = jnp.float32(0.0)
        first = group // 2 * 2
        opposite = 2 - first
        return [
            [
                jnp.where(held[0, 0] == d, codes[0, first + g], none)
                + jnp.where(held[0, 1] == d, codes[1, first + g], none)
                for g in range(2)
            ]
            for d in (group, first + 1 - core, opposite, opposite + 1)
        ]

    known = {}

    def push(k, source, target, kind, to):
        pltpu.make_async_remote_copy(
            src_ref=source,
            dst_ref=target,
            send_sem=misc.at[4 + 3 * k],
            recv_sem=misc.at[5 + 3 * k + kind],
            device_id=to,
            device_id_type=MESH,
        ).start()

    def step_params(k, _):
        if not known:
            for g, sem in ((core, misc.at[0]), (1 - core, misc.at[1])):
                arrived(state.at[g], sem)
            known["weights"] = weights()
        finish(k, 0, len(UNITS[k]) - 1)
        finish(k, 1, len(RANGES[k]) - 1)
        finish(k, 2, 0)
        new, sums, beside, landed = bufs[k][8:]
        each = sum(CHUNKS[k][1]) // 2
        mine = pl.ds(CHUNKS[k][0], each)
        first_fix = 1.0 - 0.9**10
        second_fix = 1.0 - 0.95**10
        new_params = []
        for g in range(2):
            gradient = bufs[k][0].at[OWN, OWN, OWN, pl.ds(g * each, each)][...]
            values = state.at[g, 0, mine][...]
            first_moment = 0.9 * state.at[g, 1, mine][...] + 0.1 * gradient
            second_moment = 0.95 * state.at[g, 2, mine][...] + 0.05 * gradient * gradient
            update = first_moment / first_fix / (jnp.sqrt(second_moment / second_fix) + 1e-08) + 0.1 * values
            new_params.append(values - 0.05 * update)
            new.at[g, 0][...] = new_params[g]
            new.at[g, 1][...] = first_moment
            new.at[g, 2][...] = second_moment
        total = lambda w: w[0] * new_params[0] + w[1] * new_params[1]
        by_device = known["weights"]
        for c in (1, 0):
            sums.at[2 + c][...] = total(by_device[2 + c])
        push(k, sums.at[3], landed.at[core], 1, across[1])
        known["order"] = known.get("order", []) + [k]
        if len(known["order"]) == len(CHUNKS):
            for j in known["order"]:
                push(j, bufs[j][9].at[2], bufs[j][11].at[core], 1, across[0])
        sums.at[1][...] = total(by_device[1])
        push(k, sums.at[1], beside.at[3], 0, other_core)
        push(k, new.at[1 - core], beside.at[pl.ds(0, 3)], 0, other_core)
        sums.at[0][...] = total(by_device[0])
        place = rows_in(k, core)
        for i in range(3):
            results.at[i, place][...] = new.at[core, i][...]

    def rows_in(k, which):
        return pl.ds(pl.multiple_of(which * HALF + CHUNKS[k][0], 8), sum(CHUNKS[k][1]) // 2)

    def parity(k, _):
        new, sums, beside, landed = bufs[k][8:]
        arrived(beside, misc.at[5 + 3 * k])
        place, other = rows_in(k, core), rows_in(k, 1 - core)
        for i in range(3):
            results.at[i, other][...] = beside.at[i][...]
        arrived(landed, misc.at[6 + 3 * k])
        results.at[3, place][...] = sums.at[0][...] + landed.at[core][...]
        results.at[3, other][...] = beside.at[3][...] + landed.at[1 - core][...]

    steps = {
        "l": load,
        "g": lambda k, u: give_peer(k, UNITS[k][u], (FAR,), given(k, 0, u)),
        "h": lambda k, u: give_peer(k, UNITS[k][u], (AFTER, BEFORE), given(k, 1, u)),
        "G": lambda k, g: give_peer(k, LOADS[k][g], (OWN,), given(k, 2, g)),
        "b": lambda k, u: send_raw(k, u) if (k, u) == RAW else send_far(k, 0, u),
        "x": hand_over,
        "c": lambda k, u: send_near(k, 0, u),
        "d": lambda k, u: pass_on(k, 0, u),
        "o": lambda k, u: finish(k, 0, u),
        "F": lambda k, u: send_far(k, 1, u),
        "N": lambda k, u: send_near(k, 1, u),
        "D": lambda k, u: pass_on(k, 1, u),
        "O": lambda k, u: finish(k, 1, u),
        "f": lambda k, u: send_far(k, 2, u),
        "n": lambda k, u: send_near(k, 2, u),
        "e": lambda k, u: pass_on(k, 2, u),
        "q": step_params,
        "t": parity,
    }

    barrier = pltpu.get_barrier_semaphore()
    for to in ahead + behind + [other_core, across_other]:
        pl.semaphore_signal(barrier, inc=1, device_id=to, device_id_type=MESH)
    for g in range(len(LOADS[0])):
        load(0, g)
    own_half, other_half = (pl.ds(pl.multiple_of(c * HALF, 8), HALF) for c in (core, 1 - core))
    for i, ref in enumerate((params, one, two)):
        pltpu.make_async_copy(ref.at[own_half], state.at[core, i], misc.at[0]).start()
    pltpu.make_async_copy(coding, codes, misc.at[2]).start()
    pltpu.make_async_copy(holders, held, misc.at[3]).start()
    pl.semaphore_wait(barrier, 8)
    plan = " ".join(PLAN).split()
    state_at = 12
    for number, step in enumerate(plan):
        if number == state_at:
            for i, ref in enumerate((params, one, two)):
                pltpu.make_async_remote_copy(
                    src_ref=ref.at[other_half],
                    dst_ref=state.at[core, i],
                    send_sem=misc.at[4 + 3 * len(CHUNKS)],
                    recv_sem=misc.at[1],
                    device_id=other_core,
                    device_id_type=MESH,
                ).start()
        if step[1] == "t" and step == [s for s in plan if s[1] == "t"][-1]:
            arrived(state.at[0], misc.at[4 + 3 * len(CHUNKS)])
            arrived(at(early, (), UNITS[RAW[0]][RAW[1]]), misc.at[5 + 3 * len(CHUNKS)])
            for k in range(len(CHUNKS)):
                arrived(bufs[k][0], peer_send.at[k])
                arrived(bufs[k][0].at[pl.ds(0, 3)], link_send.at[3 * k])
                arrived(bufs[k][0].at[pl.ds(0, 3), 0], link_send.at[3 * k + 1])
                arrived(bufs[k][0].at[pl.ds(0, 3), 0, 0], link_send.at[3 * k + 2])
        steps[step[1]](int(step[0]), int(step[2]) - 1)
    for k in range(len(CHUNKS)):
        arrived(bufs[k][8], misc.at[4 + 3 * k])


def write(results, *rest):
    outs, sems = rest[:-1], rest[-1]
    copies = [pltpu.make_async_copy(results.at[i], out, sems.at[i]) for i, out in enumerate(outs)]
    for copy in copies:
        copy.start()
    for copy in copies:
        copy.wait()


def shards(grads, params, moment_one, moment_two, coding, holders):
    rows = grads.shape[2] // LANES
    partial = grads.reshape(4, rows, LANES).transpose(1, 0, 2)
    flat = lambda t: t.reshape(ROWS, LANES)
    anywhere = pl.BlockSpec(memory_space=pltpu.HBM)
    vmem = pl.BlockSpec(memory_space=pltpu.VMEM)
    f32 = jnp.float32
    scratch = []
    for _, sizes in CHUNKS:
        n = sum(sizes)
        for lead in ((4, 4, 4), (4, 4, 4), (4, 4), (2, 4, 4), (4,), (2, 4), (), (2,)):
            scratch.append(pltpu.VMEM(lead + (n, LANES), f32))
        for lead in ((2, 3), (4,), (4,), (2,)):
            scratch.append(pltpu.VMEM(lead + (n // 2, LANES), f32))
    chunks = len(CHUNKS)
    scratch += [
        pltpu.VMEM((2, 3, HALF, LANES), f32),
        pltpu.VMEM((4, 4, sum(CHUNKS[RAW[0]][1]), LANES), f32),
        pltpu.VMEM((4, 4, sum(CHUNKS[RAW[0]][1]), LANES), f32),
        pltpu.SMEM((2, 4), f32),
        pltpu.SMEM((1, 2), jnp.int32),
        pltpu.SemaphoreType.DMA((chunks * 3,)),
        pltpu.SemaphoreType.DMA((sum(LANDINGS),)),
        pltpu.SemaphoreType.DMA((sum(LOADED),)),
        pltpu.SemaphoreType.DMA((sum(GIVEN),)),
        pltpu.SemaphoreType.DMA((chunks,)),
        pltpu.SemaphoreType.DMA((8 + 3 * chunks,)),
    ]
    results = pl.pallas_call(
        kernel,
        out_shape=pltpu.VMEM((4, ROWS, LANES), f32),
        in_specs=[anywhere] * 6,
        out_specs=vmem,
        scratch_shapes=scratch,
        compiler_params=pltpu.CompilerParams(
            collective_id=0, has_side_effects=True, vmem_limit_bytes=56 * 1024 * 1024
        ),
    )(partial, flat(params), flat(moment_one), flat(moment_two), coding.T, holders)
    out = pl.pallas_call(
        write,
        out_shape=[jax.ShapeDtypeStruct((ROWS, LANES), f32)] * 4,
        in_specs=[vmem],
        out_specs=[anywhere] * 4,
        scratch_shapes=[pltpu.SemaphoreType.DMA((4,))],
    )(pltpu.with_memory_space_constraint(results, pltpu.VMEM))
    return tuple(t.reshape(1, ROWS * LANES) for t in out)


def solution(mesh):
    return jax.shard_map(
        shards,
        mesh=mesh,
        in_specs=(
            P(("group", "fsdp"), None, None),
            P("group", "fsdp"),
            P("group", "fsdp"),
            P("group", "fsdp"),
            P(),
            P("fsdp", None),
        ),
        out_specs=(P("group", "fsdp"), P("group", "fsdp"), P("group", "fsdp"), P("group", "fsdp")),
        check_vma=False,
    )
```

```python
import jax
import jax.numpy as jnp
from jax import lax
from jax.experimental import pallas as pl
from jax.experimental.pallas import tpu as pltpu
from jax.sharding import PartitionSpec as P

MESH = pl.DeviceIdType.MESH
LANES = 128
ROWS = 256
STEP = (2, 3, 1, 0)
FAR, BEFORE, AFTER, OWN = range(4)
ORDERS = ((0, 1, 2), (1, 2, 0), (2, 0, 1), (2, 1, 0))
HALF = ROWS // 2
CHUNKS = ((0, (64, 64, 48, 16)), (96, (24, 16, 16, 8)))
FINE = (
    ((0, 1), (0, 1)),
    ((0, 1), (1, 2)),
    ((1, 2), (0, 1)),
    ((1, 2), (1, 2)),
    ((0, 1), (3, 1)),
    ((3, 1), (0, 1)),
    ((3, 1), (1, 2)),
    ((1, 2), (3, 1)),
    ((3, 1), (3, 1)),
)
COARSE = (((0, 3), (0, 3)), ((0, 3), (3, 1)), ((3, 1), (0, 3)), ((3, 1), (3, 1)))
UNITS = (FINE, COARSE,)
RANGES = tuple((((0, 1),), ((1, 2),), ((3, 1),)) if units is FINE else (((0, 3),), ((3, 1),)) for units in UNITS)
STAGES = tuple((units, ranges, ((),)) for units, ranges in zip(UNITS, RANGES))
LOADS = (
    (((0, 1), (0, 1)), ((0, 1), (1, 3)), ((1, 2), (0, 4)), ((3, 1), (0, 4))),
    (((0, 4), (0, 4)),),
)


def load_of(k, u):
    inside = lambda small, big: all(b[0] <= s[0] and s[0] + s[1] <= b[0] + b[1] for s, b in zip(small, big))
    return [inside(UNITS[k][u], group) for group in LOADS[k]].index(True)


LANDINGS = [2 * sum(len(units) for units in stages) for stages in STAGES]
GIVEN = [2 * len(units) + len(loads) for units, loads in zip(UNITS, LOADS)]
LOADED = [len(loads) for loads in LOADS]
RAW = (0, 1)
PLAN = (
    "0b2 0g4 0g1 0h2",
    "1g1 0h4 0G2 0b4",
    "1l1 0g6 0h1 0G3",
    "0b1 0c2 1b1 0g3",
    "1h1 0c4 0G1 0x2",
    "1g3 0h6 1G1 0g5",
    "0b6 0d4 0d2 0h3",
    "0G4 1g2 1h3 0g8",
    "0c1 0d1 0h5 0g7",
    "0b3 1h2 1g4 0h8",
    "1c1 1d1 0g9 0h7",
    "1h4 0h9 0o2 0F2",
    "1b3 0o4 0N2 0o1",
    "0F1 0c6 0d6 0b5",
    "0c3 0d3 1o1 1F1",
    "1N1 0D2 1b2 1c3",
    "1d3 0b8 0o6 0c5",
    "0d5 0b7 0o3 0N1",
    "0D1 1D1 1c2 1b4",
    "0c8 1d2 1o3 0b9",
    "0c7 0d8 0o5 0F3",
    "0d7 0O1 0f1 1O1",
    "1f1 1n1 1c4 1d4",
    "0c9 1o2 1F2 1N2",
    "0d9 0o8 0N3 0D3",
    "0o7 0O2 0n1 0e1",
    "1e1 1D2 0q1 1q1",
    "1t1 0t1",
)


def device(x, y, z, core):
    return {"group": y % 2 * 2 + core, "fsdp": y // 2 * 16 + x * 4 + z}


def kernel(grads, params, one, two, coding, holders, results, *scratch):
    bufs = [scratch[12 * k : 12 * k + 12] for k in range(len(CHUNKS))]
    state, early, late, codes, held, link_send, link_recv, own_sem, peer_sem, peer_send, misc = scratch[12 * len(CHUNKS) :]
    group, fsdp = lax.axis_index("group"), lax.axis_index("fsdp")
    core = group % 2
    here = (fsdp // 4 % 4, fsdp // 16 * 2 + group // 2, fsdp % 4)

    def along(axis, distance):
        there = list(here)
        there[axis] = (there[axis] + distance) % 4
        return device(*there, core)

    ahead = [along(axis, 1) for axis in range(3)]
    behind = [along(axis, 3) for axis in range(3)]
    other_core = device(*here, 1 - core)
    across = [device(here[0], here[1] // 2 * 2 + 1 - here[1] % 2, here[2], c) for c in range(2)]
    across_other = device(here[0], here[1] // 2 * 2 + 1 - here[1] % 2, here[2], 1 - core)

    places = [[(here[axis] + d) % 4 for d in STEP] for axis in range(3)]
    starts = (
        [v * (4 * ROWS) for v in places[0]],
        [v // 2 * (16 * ROWS) for v in places[1]],
        [v * ROWS for v in places[2]],
    )
    group_rows = [v % 2 * 2 for v in places[1]]

    def parts_of(k, odd=0):
        first, sizes = CHUNKS[k]
        out, at_row = [], 0
        for order, rows in zip(ORDERS, sizes):
            if rows == 0:
                continue
            cut = 8 * ((rows // 8 + odd) // 2)
            out.append((order, at_row, at_row + cut, at_row + rows, first + at_row))
            at_row += rows
        return out

    def slots_of(unit):
        out = [()]
        for first, count in unit:
            out = [s + (i,) for s in out for i in range(first, first + count)]
        return out

    def at(ref, lead, unit, rows=None):
        index = tuple(lead) + tuple(pl.ds(first, count) for first, count in unit)
        if rows is not None:
            index += (pl.ds(rows[0], rows[1] - rows[0]),)
        return ref.at[index] if index else ref

    def arrived(ref, sem):
        pltpu.make_async_copy(ref, ref, sem).wait()

    def terms(k, slots, which, odd=0, way=None):
        each = sum(CHUNKS[k][1]) // 2
        for order, low, cut, high, first in parts_of(k, odd):
            if way is not None:
                low, high = ((low, cut), (cut, high))[way]
            slot = {axis: slots[i] for i, axis in enumerate(order)}
            start = starts[0][slot[0]] + starts[1][slot[1]] + starts[2][slot[2]] + which * HALF + CHUNKS[k][0]
            for g in range(2):
                begin, end = max(low, g * each), min(high, (g + 1) * each)
                if begin < end:
                    rows = pl.ds(pl.multiple_of(start + (begin - g * each), 8), end - begin)
                    yield grads.at[rows, group_rows[slot[1]] + g], slots + (pl.ds(begin, end - begin),), order[0]

    def load(k, g):
        for m in range(4):
            for s in slots_of(LOADS[k][g]):
                for source, place, _ in terms(k, (m,) + s, core):
                    pltpu.make_async_copy(source, bufs[k][0].at[place], own_sem.at[sum(LOADED[:k]) + g]).start()

    def give_peer(k, block, slots, sem):
        for m in slots:
            for s in slots_of(block):
                for source, place, _ in terms(k, (m,) + s, 1 - core):
                    pltpu.make_async_remote_copy(
                        src_ref=source,
                        dst_ref=bufs[k][1].at[place],
                        send_sem=peer_send.at[k],
                        recv_sem=sem,
                        device_id=other_core,
                        device_id_type=MESH,
                    ).start()

    def given(k, kind, i):
        return peer_sem.at[sum(GIVEN[:k]) + kind * len(UNITS[k]) + i]

    waited = set()

    def ready(k, u, kind):
        g = load_of(k, u)
        if (k, g) not in waited:
            waited.add((k, g))
            arrived(at(bufs[k][0], (), ((0, 4),) + LOADS[k][g]), own_sem.at[sum(LOADED[:k]) + g])
        if kind < 2:
            slots = ((0, 1), (1, 2))[kind]
            arrived(at(bufs[k][1], (), (slots,) + UNITS[k][u]), given(k, kind, u))
        elif (k, g, OWN) not in waited:
            waited.add((k, g, OWN))
            arrived(at(bufs[k][1], (OWN,), LOADS[k][g]), given(k, 2, g))

    def add(refs):
        total = refs[0][...]
        for ref in refs[1:]:
            total = total + ref[...]
        refs[0][...] = total

    def landing(k, stage, u, kind):
        return link_recv.at[sum(LANDINGS[:k]) + 2 * (sum(len(units) for units in STAGES[k][:stage]) + u) + kind]

    def send(k, stage, u, kind, source, target, to):
        pltpu.make_async_remote_copy(
            src_ref=source,
            dst_ref=target,
            send_sem=link_send.at[3 * k + stage],
            recv_sem=landing(k, stage, u, kind),
            device_id=to,
            device_id_type=MESH,
        ).start()

    def values(k, stage, u, slot, rows):
        return at(bufs[k][0], (OWN,) * stage + (slot,), STAGES[k][stage][u], rows)

    def far(k, stage, u, rows=None):
        return at(bufs[k][2 + 2 * stage], (), STAGES[k][stage][u], rows)

    def near(k, stage, u, way, rows=None):
        return at(bufs[k][3 + 2 * stage], (way,), STAGES[k][stage][u], rows)

    def sum_up(k, stage, u, slot, rows, others):
        lead = (OWN,) * stage + (slot,)
        here_rows = (pl.ds(rows[0], rows[1] - rows[0]),)
        for s in slots_of(STAGES[k][stage][u]):
            refs = [bufs[k][0].at[lead + s + here_rows]]
            if stage == 0:
                refs.append(bufs[k][1].at[lead + s + here_rows])
            refs += [ref.at[extra + s + here_rows] for ref, extra in others]
            if len(refs) > 1:
                add(refs)

    def send_far(k, stage, u):
        whole = (0, sum(CHUNKS[k][1]))
        if stage == 0:
            ready(k, u, 0)
        sum_up(k, stage, u, FAR, whole, [])
        for order, low, cut, high, _ in parts_of(k, u % 2):
            axis = order[stage]
            for rows, to in (((low, cut), ahead[axis]), ((cut, high), behind[axis])):
                if rows[0] == rows[1]:
                    continue
                send(k, stage, u, 0, values(k, stage, u, FAR, rows), far(k, stage, u, rows), to)

    def send_raw(k, u):
        for which, target, kinds in (
            (core, bufs[k][2], (link_send.at[3 * k], landing(k, 0, u, 0))),
            (1 - core, early, (misc.at[5 + 3 * len(CHUNKS)], misc.at[6 + 3 * len(CHUNKS)])),
        ):
            for s in slots_of(UNITS[k][u]):
                for way, to in enumerate((ahead, behind)):
                    for source, place, axis in terms(k, (FAR,) + s, which, u % 2, way):
                        pltpu.make_async_remote_copy(
                            src_ref=source,
                            dst_ref=target.at[place[1:]],
                            send_sem=kinds[0],
                            recv_sem=kinds[1],
                            device_id=to[axis],
                            device_id_type=MESH,
                        ).start()

    def hand_over(k, u):
        arrived(at(early, (), UNITS[k][u]), misc.at[6 + 3 * len(CHUNKS)])
        pltpu.make_async_remote_copy(
            src_ref=at(early, (), UNITS[k][u]),
            dst_ref=at(late, (), UNITS[k][u]),
            send_sem=peer_send.at[k],
            recv_sem=misc.at[7 + 3 * len(CHUNKS)],
            device_id=other_core,
            device_id_type=MESH,
        ).start()

    def send_near(k, stage, u):
        if stage == 0:
            ready(k, u, 1)
        for order, low, cut, high, _ in parts_of(k, u % 2):
            axis = order[stage]
            for slot, way, rows, to in ((AFTER, 0, (cut, high), ahead[axis]), (BEFORE, 1, (low, cut), behind[axis])):
                if rows[0] == rows[1]:
                    continue
                sum_up(k, stage, u, slot, rows, [])
                send(k, stage, u, 1, values(k, stage, u, slot, rows), near(k, stage, u, way, rows), to)

    def pass_on(k, stage, u):
        arrived(far(k, stage, u), landing(k, stage, u, 0))
        came = [(bufs[k][2 + 2 * stage], ())]
        if stage == 0 and (k, u) == RAW:
            arrived(at(late, (), UNITS[k][u]), misc.at[7 + 3 * len(CHUNKS)])
            came.append((late, ()))
        for order, low, cut, high, _ in parts_of(k, u % 2):
            axis = order[stage]
            for slot, way, rows, to in ((AFTER, 0, (low, cut), ahead[axis]), (BEFORE, 1, (cut, high), behind[axis])):
                if rows[0] == rows[1]:
                    continue
                sum_up(k, stage, u, slot, rows, came)
                send(k, stage, u, 1, values(k, stage, u, slot, rows), near(k, stage, u, way, rows), to)

    def finish(k, stage, u):
        if stage == 0:
            ready(k, u, 2)
        arrived(at(bufs[k][3 + 2 * stage], (), ((0, 2),) + STAGES[k][stage][u]), landing(k, stage, u, 1))
        landed = bufs[k][3 + 2 * stage]
        sum_up(k, stage, u, OWN, (0, sum(CHUNKS[k][1])), [(landed, (0,)), (landed, (1,))])

    def weights():
        arrived(codes, misc.at[2])
        arrived(held, misc.at[3])
        none = jnp.float32(0.0)
        first = group // 2 * 2
        opposite = 2 - first
        return [
            [
                jnp.where(held[0, 0] == d, codes[0, first + g], none)
                + jnp.where(held[0, 1] == d, codes[1, first + g], none)
                for g in range(2)
            ]
            for d in (group, first + 1 - core, opposite, opposite + 1)
        ]

    known = {}

    def push(k, source, target, kind, to):
        pltpu.make_async_remote_copy(
            src_ref=source,
            dst_ref=target,
            send_sem=misc.at[4 + 3 * k],
            recv_sem=misc.at[5 + 3 * k + kind],
            device_id=to,
            device_id_type=MESH,
        ).start()

    def step_params(k, _):
        if not known:
            for g, sem in ((core, misc.at[0]), (1 - core, misc.at[1])):
                arrived(state.at[g], sem)
            known["weights"] = weights()
        finish(k, 0, len(UNITS[k]) - 1)
        finish(k, 1, len(RANGES[k]) - 1)
        finish(k, 2, 0)
        new, sums, beside, landed = bufs[k][8:]
        each = sum(CHUNKS[k][1]) // 2
        mine = pl.ds(CHUNKS[k][0], each)
        first_fix = 1.0 - 0.9**10
        second_fix = 1.0 - 0.95**10
        new_params, moments = [], []
        for g in range(2):
            gradient = bufs[k][0].at[OWN, OWN, OWN, pl.ds(g * each, each)][...]
            values = state.at[g, 0, mine][...]
            first_moment = 0.9 * state.at[g, 1, mine][...] + 0.1 * gradient
            second_moment = 0.95 * state.at[g, 2, mine][...] + 0.05 * gradient * gradient
            update = first_moment / first_fix / (jnp.sqrt(second_moment / second_fix) + 1e-08) + 0.1 * values
            new_params.append(values - 0.05 * update)
            moments.append((first_moment, second_moment))
        total = lambda w: w[0] * new_params[0] + w[1] * new_params[1]
        by_device = known["weights"]
        sums.at[3][...] = total(by_device[3])
        push(k, sums.at[3], landed.at[core], 1, across[1])
        sums.at[2][...] = total(by_device[2])
        known["order"] = known.get("order", []) + [k]
        if len(known["order"]) == len(CHUNKS):
            for j in known["order"]:
                push(j, bufs[j][9].at[2], bufs[j][11].at[core], 1, across[0])
        for g in range(2):
            new.at[g, 0][...] = new_params[g]
            new.at[g, 1][...], new.at[g, 2][...] = moments[g]
        sums.at[1][...] = total(by_device[1])
        push(k, sums.at[1], beside.at[3], 0, other_core)
        push(k, new.at[1 - core], beside.at[pl.ds(0, 3)], 0, other_core)
        sums.at[0][...] = total(by_device[0])
        place = rows_in(k, core)
        for i in range(3):
            results.at[i, place][...] = new.at[core, i][...]

    def rows_in(k, which):
        return pl.ds(pl.multiple_of(which * HALF + CHUNKS[k][0], 8), sum(CHUNKS[k][1]) // 2)

    def parity(k, _):
        new, sums, beside, landed = bufs[k][8:]
        arrived(beside, misc.at[5 + 3 * k])
        place, other = rows_in(k, core), rows_in(k, 1 - core)
        for i in range(3):
            results.at[i, other][...] = beside.at[i][...]
        arrived(landed, misc.at[6 + 3 * k])
        results.at[3, place][...] = sums.at[0][...] + landed.at[core][...]
        results.at[3, other][...] = beside.at[3][...] + landed.at[1 - core][...]

    steps = {
        "l": load,
        "g": lambda k, u: give_peer(k, UNITS[k][u], (FAR,), given(k, 0, u)),
        "h": lambda k, u: give_peer(k, UNITS[k][u], (AFTER, BEFORE), given(k, 1, u)),
        "G": lambda k, g: give_peer(k, LOADS[k][g], (OWN,), given(k, 2, g)),
        "b": lambda k, u: send_raw(k, u) if (k, u) == RAW else send_far(k, 0, u),
        "x": hand_over,
        "c": lambda k, u: send_near(k, 0, u),
        "d": lambda k, u: pass_on(k, 0, u),
        "o": lambda k, u: finish(k, 0, u),
        "F": lambda k, u: send_far(k, 1, u),
        "N": lambda k, u: send_near(k, 1, u),
        "D": lambda k, u: pass_on(k, 1, u),
        "O": lambda k, u: finish(k, 1, u),
        "f": lambda k, u: send_far(k, 2, u),
        "n": lambda k, u: send_near(k, 2, u),
        "e": lambda k, u: pass_on(k, 2, u),
        "q": step_params,
        "t": parity,
    }

    barrier = pltpu.get_barrier_semaphore()
    for to in ahead + behind + [other_core, across_other]:
        pl.semaphore_signal(barrier, inc=1, device_id=to, device_id_type=MESH)
    for g in range(len(LOADS[0])):
        load(0, g)
    own_half, other_half = (pl.ds(pl.multiple_of(c * HALF, 8), HALF) for c in (core, 1 - core))
    for i, ref in enumerate((params, one, two)):
        pltpu.make_async_copy(ref.at[own_half], state.at[core, i], misc.at[0]).start()
    pltpu.make_async_copy(coding, codes, misc.at[2]).start()
    pltpu.make_async_copy(holders, held, misc.at[3]).start()
    pl.semaphore_wait(barrier, 8)
    plan = " ".join(PLAN).split()
    state_at = 12
    for number, step in enumerate(plan):
        if number == state_at:
            for i, ref in enumerate((params, one, two)):
                pltpu.make_async_remote_copy(
                    src_ref=ref.at[other_half],
                    dst_ref=state.at[core, i],
                    send_sem=misc.at[4 + 3 * len(CHUNKS)],
                    recv_sem=misc.at[1],
                    device_id=other_core,
                    device_id_type=MESH,
                ).start()
        if step[1] == "t" and step == [s for s in plan if s[1] == "t"][-1]:
            arrived(state.at[0], misc.at[4 + 3 * len(CHUNKS)])
            arrived(at(early, (), UNITS[RAW[0]][RAW[1]]), misc.at[5 + 3 * len(CHUNKS)])
            for k in range(len(CHUNKS)):
                arrived(bufs[k][0], peer_send.at[k])
                arrived(bufs[k][0].at[pl.ds(0, 3)], link_send.at[3 * k])
                arrived(bufs[k][0].at[pl.ds(0, 3), 0], link_send.at[3 * k + 1])
                arrived(bufs[k][0].at[pl.ds(0, 3), 0, 0], link_send.at[3 * k + 2])
        steps[step[1]](int(step[0]), int(step[2]) - 1)
    for k in range(len(CHUNKS)):
        arrived(bufs[k][8], misc.at[4 + 3 * k])


def write(results, *rest):
    outs, sems = rest[:-1], rest[-1]
    copies = [pltpu.make_async_copy(results.at[i], out, sems.at[i]) for i, out in enumerate(outs)]
    for copy in copies:
        copy.start()
    for copy in copies:
        copy.wait()


def shards(grads, params, moment_one, moment_two, coding, holders):
    rows = grads.shape[2] // LANES
    partial = grads.reshape(4, rows, LANES).transpose(1, 0, 2)
    flat = lambda t: t.reshape(ROWS, LANES)
    anywhere = pl.BlockSpec(memory_space=pltpu.HBM)
    vmem = pl.BlockSpec(memory_space=pltpu.VMEM)
    f32 = jnp.float32
    scratch = []
    for _, sizes in CHUNKS:
        n = sum(sizes)
        for lead in ((4, 4, 4), (4, 4, 4), (4, 4), (2, 4, 4), (4,), (2, 4), (), (2,)):
            scratch.append(pltpu.VMEM(lead + (n, LANES), f32))
        for lead in ((2, 3), (4,), (4,), (2,)):
            scratch.append(pltpu.VMEM(lead + (n // 2, LANES), f32))
    chunks = len(CHUNKS)
    scratch += [
        pltpu.VMEM((2, 3, HALF, LANES), f32),
        pltpu.VMEM((4, 4, sum(CHUNKS[RAW[0]][1]), LANES), f32),
        pltpu.VMEM((4, 4, sum(CHUNKS[RAW[0]][1]), LANES), f32),
        pltpu.SMEM((2, 4), f32),
        pltpu.SMEM((1, 2), jnp.int32),
        pltpu.SemaphoreType.DMA((chunks * 3,)),
        pltpu.SemaphoreType.DMA((sum(LANDINGS),)),
        pltpu.SemaphoreType.DMA((sum(LOADED),)),
        pltpu.SemaphoreType.DMA((sum(GIVEN),)),
        pltpu.SemaphoreType.DMA((chunks,)),
        pltpu.SemaphoreType.DMA((8 + 3 * chunks,)),
    ]
    results = pl.pallas_call(
        kernel,
        out_shape=pltpu.VMEM((4, ROWS, LANES), f32),
        in_specs=[anywhere] * 6,
        out_specs=vmem,
        scratch_shapes=scratch,
        compiler_params=pltpu.CompilerParams(
            collective_id=0, has_side_effects=True, vmem_limit_bytes=56 * 1024 * 1024
        ),
    )(partial, flat(params), flat(moment_one), flat(moment_two), coding.T, holders)
    out = pl.pallas_call(
        write,
        out_shape=[jax.ShapeDtypeStruct((ROWS, LANES), f32)] * 4,
        in_specs=[vmem],
        out_specs=[anywhere] * 4,
        scratch_shapes=[pltpu.SemaphoreType.DMA((4,))],
    )(pltpu.with_memory_space_constraint(results, pltpu.VMEM))
    return tuple(t.reshape(1, ROWS * LANES) for t in out)


def solution(mesh):
    return jax.shard_map(
        shards,
        mesh=mesh,
        in_specs=(
            P(("group", "fsdp"), None, None),
            P("group", "fsdp"),
            P("group", "fsdp"),
            P("group", "fsdp"),
            P(),
            P("fsdp", None),
        ),
        out_specs=(P("group", "fsdp"), P("group", "fsdp"), P("group", "fsdp"), P("group", "fsdp")),
        check_vma=False,
    )
```
